256 devices in a mesh: shard: 16 (over y, x), grp: 16 (over z, core).
Axes of the slice: x: 4, y: 4, z: 8, core: 2. Of those that a mesh axis runs over, the one named last changes fastest.
Arguments:
- embedding: bfloat16 [65536, 768], P(('shard', 'grp'))
- cluster_id: int32 [65536], P(('shard', 'grp')), may hold values from 0 to 63, as said below
- member_order: int32 [65536], P(('shard', 'grp')), may hold values from 0 to 65535, each once
Outputs:
- nearest_earlier: float32 [65536], P(('shard', 'grp'))
The draws below stay inside these ranges and needn't reach their ends.
Inputs may be any that keep to these rules, and one draw needn't show every extreme that they name: `cluster_id`: the rows of cluster c are kept by owner shard c // 4. Of the rows of one device, at most 40 belong to one owner shard, and exactly 40 to some owner shard. Across the devices that share an index along grp, exactly 256 rows belong to each owner shard.
All inputs are finite; a program needn't handle non-finite values.
Results may differ from the reference program's by a relative error of at most 0.00068.
Values may be sent and summed in bfloat16 or wider, within the bound.
A program may use at most 64 MiB of HBM per device.

```python
import jax
import jax.numpy as jnp
from jax import lax

D = 768
ROW_DEV = 256
CLUST_OWN = 4
CAP = 40
CLUSTERS = 64
ROWS = 65536
N_SHARD = 16
N_GRP = 16


def cluster_layout(key):
    base_key = jax.random.fold_in(key, 101)
    keys_all = jax.random.split(base_key, 4)
    rest_rows = ROW_DEV - CAP
    fill_base = rest_rows // (N_SHARD - 1)
    extra_rows = rest_rows - fill_base * (N_SHARD - 1)

    def pattern(grp_key):
        first_key, second_key = jax.random.split(grp_key)
        shifts = jax.random.randint(first_key, (N_SHARD - 1,), 0, fill_base + 1)
        middle = fill_base + shifts - jnp.roll(shifts, 1) + (jnp.arange(N_SHARD - 1) < extra_rows).astype(jnp.int32)
        pattern_full = jnp.concatenate([jnp.full((1,), CAP, jnp.int32), middle.astype(jnp.int32)])
        return jax.random.permutation(second_key, pattern_full)
    patterns = jax.vmap(pattern)(jax.random.split(keys_all[0], N_GRP))
    shard_index = jnp.arange(N_SHARD)
    offsets = (shard_index[None, :] - shard_index[:, None]) % N_SHARD
    counts = jnp.transpose(patterns[:, offsets], (1, 0, 2))
    boundary = jnp.cumsum(counts, axis=-1)
    positions = jnp.arange(ROW_DEV)
    owner_seq = jnp.sum((boundary[:, :, None, :] <= positions[:, None]).astype(jnp.int32), axis=-1)
    shuffles = jax.vmap(lambda sub_key: jax.random.permutation(sub_key, ROW_DEV))(jax.random.split(keys_all[1], N_SHARD * N_GRP))
    shuffles = shuffles.reshape(N_SHARD, N_GRP, ROW_DEV)
    owner_rows = jnp.take_along_axis(owner_seq, shuffles, axis=-1).reshape(ROWS)
    first_pick = jax.random.randint(keys_all[2], (ROWS,), 0, CLUST_OWN)
    second_pick = jax.random.randint(jax.random.fold_in(keys_all[2], 1), (ROWS,), 0, CLUST_OWN)
    local_index = jnp.minimum(first_pick, second_pick)
    clusters = (owner_rows * CLUST_OWN + local_index).astype(jnp.int32)
    per_cluster = max(ROWS // (4 * CLUSTERS), 1)
    templates = jax.random.randint(keys_all[3], (ROWS,), 0, per_cluster)
    return (clusters, templates)


def draw_cluster_id(key, part):
    layout = cluster_layout(key)
    return layout[0]


def draw_embedding(key, part):
    clusters, templates = cluster_layout(key)
    key = jax.random.fold_in(key, 7)
    subkeys = jax.random.split(key, 4)
    per_cluster = max(ROWS // (4 * CLUSTERS), 1)
    centers = jax.random.normal(subkeys[0], (CLUSTERS, D), jnp.float32)
    template_table = jax.random.normal(subkeys[1], (CLUSTERS * per_cluster, D), jnp.float32)
    jitter = jax.random.normal(subkeys[2], (ROWS, D), jnp.float32)
    uniform_part = jax.random.uniform(subkeys[3], (ROWS, 1), jnp.float32, 0.0, 1.0)
    mixing = 2.0 * uniform_part * uniform_part
    combined = 0.5 * centers[clusters] + mixing * template_table[clusters * per_cluster + templates] + jitter
    return combined.astype(jnp.bfloat16)


def setup_inputs(seed: int = 0) -> dict:
    arg_keys = jax.random.split(jax.random.key(seed), 4)
    return {
        "embedding": draw_embedding(jax.random.fold_in(arg_keys[3], 71), 0),
        "cluster_id": draw_cluster_id(jax.random.fold_in(arg_keys[3], 71), 0),
        "member_order": jax.random.permutation(arg_keys[2], ROWS).astype(jnp.int32),
    }


def reference(embedding, cluster_id, member_order):
    widened = embedding.astype(jnp.float32)
    squares = lax.optimization_barrier(lax.optimization_barrier(jnp.sum(widened * widened, axis=1, keepdims=True)))
    normed = (widened * lax.rsqrt(squares + 1e-06)).astype(jnp.bfloat16)
    owner_shard = (cluster_id // CLUST_OWN).astype(jnp.int32)
    arrangement = jnp.argsort(owner_shard, stable=True).astype(jnp.int32)
    group_rows = N_GRP * ROW_DEV
    grouped = normed[arrangement].reshape(N_SHARD, group_rows, D)
    grouped_cluster = cluster_id[arrangement].reshape(N_SHARD, group_rows)
    grouped_rank = member_order[arrangement].reshape(N_SHARD, group_rows)

    def per_owner(inputs):
        member_rows, member_cluster, member_rank = inputs
        scores = jnp.dot(member_rows, member_rows.T, preferred_element_type=jnp.float32)
        allowed = (member_cluster[:, None] == member_cluster[None, :]) & (member_rank[None, :] < member_rank[:, None])
        return lax.optimization_barrier(jnp.max(jnp.where(allowed, scores, -1.0), axis=1))
    found_max = lax.map(per_owner, (grouped, grouped_cluster, grouped_rank))
    return jnp.zeros((ROWS,), jnp.float32).at[arrangement].set(found_max.reshape(-1))
```

```python
import functools

import jax
import jax.numpy as jnp
from jax import lax
from jax.experimental import pallas as pl
from jax.experimental.pallas import tpu as pltpu
from jax.sharding import PartitionSpec as P

MESH = pl.DeviceIdType.MESH
HIGHEST = lax.Precision.HIGHEST
CLUST_OWN = 4
SIDE = 4
RANKS = 65536

T0, TP1, TM1, TP2, TM2, U0, UM1, UM2 = range(8)
PP1, PM1, PP2, PU0, PUM1 = range(5)


def iota(shape, dim):
    return lax.broadcasted_iota(jnp.int32, shape, dim)


def one_hot(cond, dtype=jnp.bfloat16):
    return jnp.where(cond, 1.0, 0.0).astype(dtype)


def dot_nt(a, b, precision=None):
    return lax.dot_general(
        a, b, (((1,), (1,)), ((), ())), preferred_element_type=jnp.float32, precision=precision
    )


def dot_nn(a, b, precision=None):
    return lax.dot_general(
        a, b, (((1,), (0,)), ((), ())), preferred_element_type=jnp.float32, precision=precision
    )


def kernel(
    shards,
    capacity,
    emb_ref,
    cid_ref,
    rank_ref,
    out_ref,
    send_buf,
    recv_buf,
    blk,
    meta_send,
    meta_recv,
    zmeta,
    kcol,
    part_send,
    part_recv,
    ret_send,
    ret_recv,
    xy_send,
    xy_recv,
    meta_ssem,
    meta_rsem,
    z_send,
    z_recv,
    zm_send,
    zm_recv,
    p_send,
    p_recv,
    r_send,
    r_recv,
):
    row_dev = emb_ref.shape[0]
    chunks = blk.shape[1]
    width = blk.shape[3]
    half = width // 2
    me = lax.axis_index("shard")
    grp = lax.axis_index("grp")
    y, x = me // SIDE, me % SIDE
    z, core = grp // 2, grp % 2
    n_z = lax.axis_size("grp") // 2

    def xy_dev(k, sign):
        dy, dx = k // SIDE, k % SIDE
        py = (y + sign * dy + SIDE) % SIDE
        px = (x + sign * dx + SIDE) % SIDE
        return (py * SIDE + px, grp)

    def z_dev(dz, other):
        pc = 1 - core if other else core
        return (me, ((z + dz + n_z) % n_z) * 2 + pc)

    barrier = pltpu.get_barrier_semaphore()
    for k in range(1, shards):
        pl.semaphore_signal(barrier, inc=1, device_id=xy_dev(k, 1), device_id_type=MESH)
    column = [(d, o) for d in (-2, -1, 0, 1, 2) for o in (False, True) if (d, o) != (0, False)]
    for d, o in column:
        pl.semaphore_signal(barrier, inc=1, device_id=z_dev(d, o), device_id_type=MESH)

    def remote(src, dst, ssem, rsem, dev):
        copy = pltpu.make_async_remote_copy(
            src_ref=src, dst_ref=dst, send_sem=ssem, recv_sem=rsem, device_id=dev, device_id_type=MESH
        )
        copy.start()

    def arrived(ref, sem):
        pltpu.make_async_copy(ref, ref, sem).wait()

    cid = cid_ref[...]
    owner = cid // CLUST_OWN
    rel = ((owner // SIDE - y + SIDE) % SIDE) * SIDE + (owner % SIDE - x + SIDE) % SIDE
    is_owner = iota((shards, row_dev), 0) == rel
    earlier = one_hot(iota((row_dev, row_dev), 0) < iota((row_dev, row_dev), 1))
    before = dot_nn(one_hot(is_owner), earlier)
    slot = jnp.sum(jnp.where(is_owner, before, 0.0), axis=0, keepdims=True).astype(jnp.int32)
    target = rel * capacity + slot
    pack = one_hot(iota((shards * capacity, row_dev), 0) == target)

    key_own = (cid * RANKS + rank_ref[...] + 1).astype(jnp.float32)
    row_no = (iota((1, row_dev), 1) + 1).astype(jnp.float32)
    lane_k = iota((128, row_dev), 0)
    meta = dot_nt(
        jnp.where(is_owner, key_own, 0.0), one_hot(lane_k == slot, jnp.float32), HIGHEST
    ) + dot_nt(
        jnp.where(is_owner, row_no, 0.0), one_hot(lane_k == slot + 64, jnp.float32), HIGHEST
    )
    meta_recv[0] = meta[0:1]
    for k in range(1, shards):
        meta_send[k] = meta[k : k + 1]

    wide = emb_ref[...].astype(jnp.float32)
    normed = (
        wide * lax.rsqrt(jnp.sum(wide * wide, axis=1, keepdims=True) + 1e-06)
    ).astype(jnp.bfloat16)

    def pack_chunk(q):
        rows = dot_nn(pack, normed[:, q * width : (q + 1) * width])
        rows = rows.reshape(shards, capacity, width)
        rows = jnp.concatenate([rows[:, :, :half], rows[:, :, half:]], axis=1).astype(jnp.bfloat16)
        recv_buf[q, 0] = rows[0]
        send_buf[q, 1:] = rows[1:]

    def send_chunk(q):
        for k in range(1, shards):
            remote(
                send_buf.at[q, k], recv_buf.at[q, k], xy_send.at[q], xy_recv.at[q], xy_dev(k, 1)
            )

    pack_chunk(0)
    pl.semaphore_wait(barrier, shards - 1 + len(column))
    for k in range(1, shards):
        remote(meta_send.at[k], meta_recv.at[k], meta_ssem, meta_rsem, xy_dev(k, 1))
    send_chunk(0)
    for q in range(1, chunks):
        pack_chunk(q)
        send_chunk(q)

    arrived(meta_recv.at[pl.ds(1, shards - 1)], meta_rsem)
    got = meta_recv[...].reshape(shards, 128)
    lanes = iota((shards, 128), 1)
    count = jnp.sum(jnp.where((got > 0.0) & (lanes < 64), 1.0, 0.0), axis=1, keepdims=True)
    lower = iota((shards, shards), 1) < iota((shards, shards), 0)
    count_row = jnp.sum(
        jnp.where(iota((shards, shards), 0) == iota((shards, shards), 1), count, 0.0),
        axis=0,
        keepdims=True,
    )
    offset = jnp.sum(jnp.where(lower, count_row, 0.0), axis=1, keepdims=True)
    offset_i = offset.astype(jnp.int32)
    count_i = count.astype(jnp.int32)

    places = shards * 2 * capacity
    inner = iota((shards, places), 1) - iota((shards, places), 0) * (2 * capacity)

    def place(h):
        k = inner - h * capacity
        good = (k >= 0) & (k < jnp.minimum(count_i, capacity))
        return jnp.sum(jnp.where(good, offset_i + k + 1, 0), axis=0, keepdims=True) - 1

    pos = iota((row_dev, places), 0)
    gather = jnp.concatenate([one_hot(pos == place(0)), one_hot(pos == place(1))], axis=0)

    member = iota((shards, row_dev), 1)
    from_src = (member >= offset_i) & (member < offset_i + count_i)
    within = iota((1, row_dev), 1) - jnp.sum(
        jnp.where(from_src, offset_i, 0), axis=0, keepdims=True
    )
    got_t = jnp.concatenate([got, jnp.zeros((128 - shards, 128), jnp.float32)], axis=0).T
    from_pad = jnp.concatenate(
        [one_hot(from_src, jnp.float32), jnp.zeros((128 - shards, row_dev), jnp.float32)], axis=0
    )
    spread = dot_nn(got_t, from_pad, HIGHEST)
    key_row = jnp.sum(jnp.where(lane_k == within, spread, 0.0), axis=0, keepdims=True) - 1.0
    home_row = jnp.sum(jnp.where(lane_k == within + 64, spread, 0.0), axis=0, keepdims=True) - 1.0
    zmeta[T0] = key_row
    for slot_no, d, o in (
        (TP1, -1, False),
        (TM1, 1, False),
        (TP2, -2, False),
        (TM2, 2, False),
        (U0, 0, True),
        (UM1, 1, True),
        (UM2, 2, True),
    ):
        remote(zmeta.at[T0], zmeta.at[slot_no], zm_send, zm_recv, z_dev(d, o))

    def compact(q):
        arrived(recv_buf.at[q, pl.ds(1, shards - 1)], xy_recv.at[q])
        both = dot_nn(gather, recv_buf[q].reshape(places, half))
        blk[T0, q] = jnp.concatenate([both[:row_dev], both[row_dev:]], axis=1).astype(jnp.bfloat16)

    def z_copy(src_slot, dst_slot, q, d, o):
        remote(
            blk.at[src_slot, q],
            blk.at[dst_slot, q],
            z_send.at[dst_slot, q],
            z_recv.at[dst_slot, q],
            z_dev(d, o),
        )

    def z_wait(slot_no, q):
        arrived(blk.at[slot_no, q], z_recv.at[slot_no, q])

    def send_own(q):
        z_copy(T0, TM1, q, 1, False)
        z_copy(T0, TP1, q, -1, False)
        z_copy(T0, U0, q, 0, True)

    def forward(q):
        z_wait(TM1, q)
        z_copy(TM1, TM2, q, 1, False)
        z_copy(TM1, UM1, q, 0, True)
        z_wait(TP1, q)
        z_copy(TP1, TP2, q, -1, False)

    for q in range(chunks):
        compact(q)
        send_own(q)
        if q:
            forward(q - 1)
    forward(chunks - 1)

    arrived(zmeta.at[pl.ds(1, 7)], zm_recv)
    keys = zmeta[...].reshape(8, row_dev)
    eye = one_hot(iota((row_dev, row_dev), 0) == iota((row_dev, row_dev), 1), jnp.float32)
    keys_t = dot_nt(eye, keys, HIGHEST)
    for b in range(8):
        kcol[b] = jnp.broadcast_to(keys_t[:, b : b + 1], (row_dev, row_dev))
    first_key = jnp.floor(keys * (1.0 / RANKS)) * RANKS

    def best(query, key_slots, running=None):
        for ks in key_slots:
            scores = dot_nt(blk[ks, 0], blk[query, 0])
            for q in range(1, chunks):
                scores += dot_nt(blk[ks, q], blk[query, q])
            col = kcol[ks]
            allowed = (col < keys[query : query + 1]) & (col >= first_key[query : query + 1])
            top = jnp.max(jnp.where(allowed, scores, -1.0), axis=0, keepdims=True)
            running = top if running is None else jnp.maximum(running, top)
        return running

    def send_part(p, value, d, o):
        part_send[p] = value
        remote(part_send.at[p], part_recv.at[p], p_send, p_recv, z_dev(d, o))

    for q in range(chunks):
        z_wait(U0, q)
    mine = best(T0, (T0, U0, TP1))
    send_part(PU0, best(U0, (TP1,)), 0, True)
    for q in range(chunks):
        z_wait(TM2, q)
        z_copy(TM2, UM2, q, 0, True)
    for q in range(chunks):
        z_wait(UM1, q)
    send_part(PP1, best(TP1, (T0, U0, TM1, UM1)), 1, False)
    early_m1 = best(TM1, (TP1,))
    early_um1 = best(UM1, (TP1,))
    for q in range(chunks):
        z_wait(TP2, q)
    send_part(PM1, best(TM1, (TP2,), early_m1), -1, False)
    send_part(PUM1, best(UM1, (TP2,), early_um1), -1, True)
    late = best(TP2, (TM1, UM1, TM2))
    for q in range(chunks):
        z_wait(UM2, q)
    send_part(PP2, best(TP2, (UM2,), late), 2, False)

    arrived(part_recv, p_recv)
    mine = jnp.maximum(mine, jnp.max(part_recv[...].reshape(5, row_dev), axis=0, keepdims=True))
    back = dot_nt(
        jnp.where(from_src, mine, 0.0),
        one_hot(iota((row_dev, row_dev), 0) == home_row.astype(jnp.int32), jnp.float32),
        HIGHEST,
    )
    ret_recv[0] = back[0:1]
    for k in range(1, shards):
        ret_send[k] = back[k : k + 1]
    for k in range(1, shards):
        remote(ret_send.at[k], ret_recv.at[k], r_send, r_recv, xy_dev(k, -1))
    arrived(ret_recv.at[pl.ds(1, shards - 1)], r_recv)
    out_ref[...] = jnp.sum(ret_recv[...].reshape(shards, row_dev), axis=0, keepdims=True)

    arrived(meta_send.at[pl.ds(1, shards - 1)], meta_ssem)
    for q in range(chunks):
        arrived(send_buf.at[q, pl.ds(1, shards - 1)], xy_send.at[q])
        for b in range(1, 8):
            arrived(blk.at[b, q], z_send.at[b, q])
    arrived(zmeta.at[pl.ds(1, 7)], zm_send)
    arrived(part_send, p_send)
    arrived(ret_send.at[pl.ds(1, shards - 1)], r_send)


def per_device(embedding, cluster_id, member_order):
    shards = lax.axis_size("shard")
    row_dev, depth = embedding.shape
    capacity = 5 * row_dev // (2 * shards)
    width = 256
    chunks = depth // width
    dma = pltpu.SemaphoreType.DMA
    out = pl.pallas_call(
        functools.partial(kernel, shards, capacity),
        out_shape=jax.ShapeDtypeStruct((1, row_dev), jnp.float32),
        in_specs=[pl.BlockSpec(memory_space=pltpu.VMEM)] * 3,
        out_specs=pl.BlockSpec(memory_space=pltpu.VMEM),
        scratch_shapes=[
            pltpu.VMEM((chunks, shards, 2 * capacity, width // 2), jnp.bfloat16),
            pltpu.VMEM((chunks, shards, 2 * capacity, width // 2), jnp.bfloat16),
            pltpu.VMEM((8, chunks, row_dev, width), jnp.bfloat16),
            pltpu.VMEM((shards, 1, 128), jnp.float32),
            pltpu.VMEM((shards, 1, 128), jnp.float32),
            pltpu.VMEM((8, 1, row_dev), jnp.float32),
            pltpu.VMEM((8, row_dev, row_dev), jnp.float32),
            pltpu.VMEM((5, 1, row_dev), jnp.float32),
            pltpu.VMEM((5, 1, row_dev), jnp.float32),
            pltpu.VMEM((shards, 1, row_dev), jnp.float32),
            pltpu.VMEM((shards, 1, row_dev), jnp.float32),
            dma((chunks,)),
            dma((chunks,)),
            dma,
            dma,
            dma((8, chunks)),
            dma((8, chunks)),
            dma,
            dma,
            dma,
            dma,
            dma,
            dma,
        ],
        compiler_params=pltpu.CompilerParams(
            collective_id=0, has_side_effects=True, vmem_limit_bytes=40 * 2**20
        ),
    )(embedding, cluster_id.reshape(1, row_dev), member_order.reshape(1, row_dev))
    return out.reshape(row_dev)


def solution(mesh):
    in_specs = (P(("shard", "grp"), None), P(("shard", "grp")), P(("shard", "grp")))
    out_specs = P(("shard", "grp"))
    return jax.shard_map(
        per_device, mesh=mesh, in_specs=in_specs, out_specs=out_specs, check_vma=False
    )
```

```python
import functools

import jax
import jax.numpy as jnp
from jax import lax
from jax.experimental import pallas as pl
from jax.experimental.pallas import tpu as pltpu
from jax.sharding import PartitionSpec as P

MESH = pl.DeviceIdType.MESH
HIGHEST = lax.Precision.HIGHEST
CLUST_OWN = 4
SIDE = 4
RANKS = 65536
UNIT = 128
PREPARE = 2
PLAN = (1, 1, 2, 2)

T0, TP1, TM1, TP2, TM2, U0, UM1, UM2 = range(8)
PP1, PM1, PP2, PU0, PUM1 = range(5)
DIRECT = ((TP1, TM1),)


def iota(shape, dim):
    return lax.broadcasted_iota(jnp.int32, shape, dim)


def one_hot(cond, dtype=jnp.bfloat16):
    return jnp.where(cond, 1.0, 0.0).astype(dtype)


def dot_nt(a, b, precision=None):
    return lax.dot_general(
        a, b, (((1,), (1,)), ((), ())), preferred_element_type=jnp.float32, precision=precision
    )


def dot_nn(a, b, precision=None):
    return lax.dot_general(
        a, b, (((1,), (0,)), ((), ())), preferred_element_type=jnp.float32, precision=precision
    )


def dot_whole(a, selector):
    rows = a.shape[0]
    pieces = []
    for _ in range(3):
        pieces.append(a.astype(jnp.bfloat16))
        a = a - pieces[-1].astype(jnp.float32)
    out = dot_nt(jnp.concatenate(pieces, axis=0), selector)
    return out[:rows] + out[rows : 2 * rows] + out[2 * rows :]


def kernel(shards, capacity, plan, emb_hbm, cid_hbm, rank_hbm, out_ref, *refs):
    n = len(plan)
    m = n + len(DIRECT)
    send_buf, recv_buf, refs = refs[:m], refs[m : 2 * m], refs[2 * m :]
    (
        emb_ref,
        cid_ref,
        rank_ref,
        blk,
        acc,
        meta_send,
        meta_recv,
        zmeta,
        raw,
        raw_target,
        counts,
        kcol,
        part_send,
        part_recv,
        ret_send,
        ret_recv,
        in_sem,
        xy_send,
        xy_recv,
        meta_ssem,
        meta_rsem,
        z_send,
        z_recv,
        zm_send,
        zm_recv,
        raw_ssem,
        raw_rsem,
        rt_send,
        rt_recv,
        c_send,
        c_recv,
        p_send,
        p_recv,
        r_send,
        r_recv,
    ) = refs
    row_dev = emb_ref.shape[0]
    padded = -(-capacity // 16) * 16
    first = [sum(plan[:q]) for q in range(n + 1)]
    last = first[n] - 1 if DIRECT else first[n]
    direct = [b for pair in DIRECT for b in pair]
    me = lax.axis_index("shard")
    grp = lax.axis_index("grp")
    y, x = me // SIDE, me % SIDE
    z, core = grp // 2, grp % 2
    n_z = lax.axis_size("grp") // 2

    loads = [
        pltpu.make_async_copy(src, dst, in_sem.at[a])
        for a, (src, dst) in enumerate(
            ((cid_hbm, cid_ref), (rank_hbm, rank_ref), (emb_hbm, emb_ref))
        )
    ]
    for load in loads:
        load.start()

    def xy_dev(k, sign):
        dy, dx = k // SIDE, k % SIDE
        py = (y + sign * dy + SIDE) % SIDE
        px = (x + sign * dx + SIDE) % SIDE
        return (py * SIDE + px, grp)

    def z_dev(dz, other):
        pc = 1 - core if other else core
        return (me, ((z + dz + n_z) % n_z) * 2 + pc)

    barrier = pltpu.get_barrier_semaphore()
    for k in range(1, shards):
        pl.semaphore_signal(barrier, inc=1, device_id=xy_dev(k, 1), device_id_type=MESH)
    column = [(d, o) for d in (-2, -1, 0, 1, 2) for o in (False, True) if (d, o) != (0, False)]
    for d, o in column:
        pl.semaphore_signal(barrier, inc=1, device_id=z_dev(d, o), device_id_type=MESH)

    def remote(src, dst, ssem, rsem, dev):
        copy = pltpu.make_async_remote_copy(
            src_ref=src, dst_ref=dst, send_sem=ssem, recv_sem=rsem, device_id=dev, device_id_type=MESH
        )
        copy.start()

    def arrived(ref, sem):
        pltpu.make_async_copy(ref, ref, sem).wait()

    loads[0].wait()
    loads[1].wait()
    cid = cid_ref[...]
    owner = cid // CLUST_OWN
    rel = ((owner // SIDE - y + SIDE) % SIDE) * SIDE + (owner % SIDE - x + SIDE) % SIDE
    is_owner = iota((shards, row_dev), 0) == rel
    earlier = one_hot(iota((row_dev, row_dev), 0) < iota((row_dev, row_dev), 1))
    before = dot_nn(one_hot(is_owner), earlier)
    slot = jnp.sum(jnp.where(is_owner, before, 0.0), axis=0, keepdims=True).astype(jnp.int32)
    target = rel * padded + slot
    pack = one_hot(iota((shards * padded, row_dev), 0) == target)

    key_own = (cid * RANKS + rank_ref[...] + 1).astype(jnp.float32)
    row_no = (iota((1, row_dev), 1) + 1).astype(jnp.float32)
    lane_k = iota((128, row_dev), 0)
    meta = dot_whole(jnp.where(is_owner, key_own, 0.0), one_hot(lane_k == slot)) + dot_nt(
        jnp.where(is_owner, row_no, 0.0).astype(jnp.bfloat16), one_hot(lane_k == slot + 64)
    )
    meta_recv[0] = meta[0:1]
    for k in range(1, shards):
        meta_send[k] = meta[k : k + 1]

    loads[2].wait()
    wide = emb_ref[...].astype(jnp.float32)
    normed = (
        wide * lax.rsqrt(jnp.sum(wide * wide, axis=1, keepdims=True) + 1e-06)
    ).astype(jnp.bfloat16)

    if DIRECT:
        raw[T0] = normed[:, last * UNIT :]
        raw_target[T0] = target.astype(jnp.float32)
    neighbours = [bd for bd in ((TP1, -1), (TM1, 1), (TP2, -2), (TM2, 2)) if bd[0] in direct]

    def pack_chunk(q):
        rows = dot_nn(pack, normed[:, first[q] * UNIT : first[q + 1] * UNIT])
        rows = rows.reshape(shards, padded, plan[q] * UNIT)
        if plan[q] == 2:
            rows = jnp.concatenate(
                [rows[:, :capacity, :UNIT], rows[:, :capacity, UNIT:]], axis=1
            )
        rows = rows.astype(jnp.bfloat16)
        recv_buf[q][0] = rows[0]
        send_buf[q][1:] = rows[1:]

    def send_chunk(q):
        for k in range(1, shards):
            remote(
                send_buf[q].at[k], recv_buf[q].at[k], xy_send.at[q], xy_recv.at[q], xy_dev(k, 1)
            )

    pack_chunk(0)
    pl.semaphore_wait(barrier, shards - 1 + len(column))
    for k in range(1, shards):
        remote(meta_send.at[k], meta_recv.at[k], meta_ssem, meta_rsem, xy_dev(k, 1))
    send_chunk(0)
    for b, d in neighbours:
        remote(raw_target.at[T0], raw_target.at[b], rt_send, rt_recv, z_dev(d, False))
        remote(raw.at[T0], raw.at[b], raw_ssem.at[b], raw_rsem.at[b], z_dev(d, False))
    for q in range(1, n):
        pack_chunk(q)
        send_chunk(q)

    def pack_direct(e):
        halves = []
        for b in DIRECT[e]:
            arrived(raw.at[b], raw_rsem.at[b])
            to = raw_target[b].astype(jnp.int32)
            rows = dot_nn(one_hot(iota((shards * padded, row_dev), 0) == to), raw[b])
            halves.append(rows.reshape(shards, padded, UNIT)[:, :capacity])
        rows = jnp.concatenate(halves, axis=1).astype(jnp.bfloat16)
        recv_buf[n + e][0] = rows[0]
        send_buf[n + e][1:] = rows[1:]
        send_chunk(n + e)

    arrived(meta_recv.at[pl.ds(1, shards - 1)], meta_rsem)
    got = meta_recv[...].reshape(shards, 128)
    lanes = iota((shards, 128), 1)
    count = jnp.sum(jnp.where((got > 0.0) & (lanes < 64), 1.0, 0.0), axis=1, keepdims=True)
    lower = iota((shards, shards), 1) < iota((shards, shards), 0)
    count_row = jnp.sum(
        jnp.where(iota((shards, shards), 0) == iota((shards, shards), 1), count, 0.0),
        axis=0,
        keepdims=True,
    )
    offset = jnp.sum(jnp.where(lower, count_row, 0.0), axis=1, keepdims=True).astype(jnp.int32)
    count = count.astype(jnp.int32)

    def place(units, h, offset=offset, count=count):
        rows = padded if units == 1 else units * capacity
        k = iota((shards, shards * rows), 1) - iota((shards, shards * rows), 0) * rows - h * capacity
        good = (k >= 0) & (k < count)
        where_to = jnp.sum(jnp.where(good, offset + k + 1, 0), axis=0, keepdims=True) - 1
        return one_hot(iota((row_dev, shards * rows), 0) == where_to)

    gathers = {}

    def compact(q):
        units = plan[q]
        if units not in gathers:
            gathers[units] = jnp.concatenate([place(units, h) for h in range(units)], axis=0)
        arrived(recv_buf[q].at[pl.ds(1, shards - 1)], xy_recv.at[q])
        rows = recv_buf[q][...]
        out = dot_nn(gathers[units], rows.reshape(rows.shape[0] * rows.shape[1], UNIT))
        blk[T0, first[q] : first[q + 1]] = out.reshape(units, row_dev, UNIT).astype(jnp.bfloat16)

    def direct_places(e):
        places = []
        for h, b in enumerate(DIRECT[e]):
            packed = counts[b][:, :1].astype(jnp.int32)
            places.append(place(2, h, packed % 1024, packed // 1024))
        return jnp.concatenate(places, axis=0)

    def compact_direct(e):
        arrived(recv_buf[n + e].at[pl.ds(1, shards - 1)], xy_recv.at[n + e])
        rows = recv_buf[n + e][...]
        out = dot_nn(
            direct_gather[e], rows.reshape(rows.shape[0] * rows.shape[1], UNIT)
        ).astype(jnp.bfloat16)
        for h, b in enumerate(DIRECT[e]):
            blk[b, last] = out[h * row_dev : (h + 1) * row_dev]

    def z_copy(src_slot, dst_slot, u, d, o):
        remote(
            blk.at[src_slot, u],
            blk.at[dst_slot, u],
            z_send.at[dst_slot, u],
            z_recv.at[dst_slot, u],
            z_dev(d, o),
        )

    def z_wait(slot_no, u):
        arrived(blk.at[slot_no, u], z_recv.at[slot_no, u])

    def units_of(q):
        return range(first[q], first[q + 1])

    def send_own(q):
        for u in units_of(q):
            if u == last:
                continue
            z_copy(T0, TM1, u, 1, False)
            z_copy(T0, TP1, u, -1, False)
        for u in units_of(q):
            z_copy(T0, U0, u, 0, True)

    def forward(q):
        for u in units_of(q):
            if u == last:
                continue
            z_wait(TM1, u)
            z_copy(TM1, TM2, u, 1, False)
            z_copy(TM1, UM1, u, 0, True)
            z_wait(TP1, u)
            z_copy(TP1, TP2, u, -1, False)

    compact(0)
    send_own(0)

    member = iota((shards, row_dev), 1)
    from_src = (member >= offset) & (member < offset + count)
    within = iota((1, row_dev), 1) - jnp.sum(jnp.where(from_src, offset, 0), axis=0, keepdims=True)
    got_t = jnp.concatenate([got, jnp.zeros((128 - shards, 128), jnp.float32)], axis=0).T
    from_pad = jnp.concatenate(
        [one_hot(from_src, jnp.float32), jnp.zeros((128 - shards, row_dev), jnp.float32)], axis=0
    )
    spread = dot_nn(got_t, from_pad, HIGHEST)
    key_row = jnp.sum(jnp.where(lane_k == within, spread, 0.0), axis=0, keepdims=True) - 1.0
    home_row = jnp.sum(jnp.where(lane_k == within + 64, spread, 0.0), axis=0, keepdims=True) - 1.0
    counts[T0] = jnp.broadcast_to((offset + 1024 * count).astype(jnp.float32), (shards, 128))
    for b, d in neighbours:
        remote(counts.at[T0], counts.at[b], c_send, c_recv, z_dev(d, False))
    zmeta[T0] = key_row
    for slot_no, d, o in (
        (TP1, -1, False),
        (TM1, 1, False),
        (TP2, -2, False),
        (TM2, 2, False),
        (U0, 0, True),
        (UM1, 1, True),
        (UM2, 2, True),
    ):
        remote(zmeta.at[T0], zmeta.at[slot_no], zm_send, zm_recv, z_dev(d, o))

    if DIRECT:
        arrived(raw_target.at[pl.ds(1, len(direct))], rt_recv)
    for q in range(1, n):
        compact(q)
        send_own(q)
        if q <= len(DIRECT):
            pack_direct(q - 1)
        forward(q - 1)
        if q == PREPARE:
            home = one_hot(iota((row_dev, row_dev), 0) == home_row.astype(jnp.int32))
            arrived(zmeta.at[pl.ds(1, 7)], zm_recv)
            keys = zmeta[...].reshape(8, row_dev)
            eye = one_hot(iota((row_dev, row_dev), 0) == iota((row_dev, row_dev), 1), jnp.float32)
            keys_t = dot_nt(eye, keys, HIGHEST)
            for b in range(8):
                kcol[b] = jnp.broadcast_to(keys_t[:, b : b + 1], (row_dev, 128))
            first_key = jnp.floor(keys * (1.0 / RANKS)) * RANKS
            if DIRECT:
                arrived(counts.at[pl.ds(1, len(direct))], c_recv)
            direct_gather = [direct_places(e) for e in range(len(DIRECT))]
    forward(n - 1)
    if DIRECT:
        compact_direct(0)
        z_copy(TM1, UM1, last, 0, True)
        if TM2 not in direct:
            z_copy(TM1, TM2, last, 1, False)
            z_copy(TP1, TP2, last, -1, False)

    def scores(query, key, start, stop):
        total = None
        for u in range(start, stop, 2):
            take = range(u, min(u + 2, stop))
            a = jnp.concatenate([blk[key, v] for v in take], axis=1)
            b = jnp.concatenate([blk[query, v] for v in take], axis=1)
            term = dot_nt(a, b)
            total = term if total is None else total + term
        return total

    def top(query, key, total):
        col = jnp.concatenate([kcol[key]] * (row_dev // 128), axis=1)
        allowed = (col < keys[query : query + 1]) & (col >= first_key[query : query + 1])
        return jnp.max(jnp.where(allowed, total, -1.0), axis=0, keepdims=True)

    def best(query, key_slots):
        running = None
        for key in key_slots:
            found = top(query, key, scores(query, key, 0, first[n]))
            running = found if running is None else jnp.maximum(running, found)
        return running

    def send_part(p, value, d, o):
        part_send[p] = value
        remote(part_send.at[p], part_recv.at[p], p_send, p_recv, z_dev(d, o))

    all_units = range(first[n])
    tail = first[n] - 2

    def pass_on(units):
        for u in units:
            z_wait(TM2, u)
            z_copy(TM2, UM2, u, 0, True)

    pass_on(range(first[n - 2]))
    for u in all_units:
        z_wait(U0, u)
    mine = best(T0, (T0, U0, TP1))
    send_part(PU0, best(U0, (TP1,)), 0, True)
    early_p1 = best(TP1, (T0, U0, TM1))
    early_m1 = best(TM1, (TP1,))
    for u in all_units:
        z_wait(UM1, u)
    send_part(PP1, jnp.maximum(early_p1, best(TP1, (UM1,))), 1, False)
    early_um1 = best(UM1, (TP1,))
    pass_on(range(first[n - 2], tail))
    if len(DIRECT) > 1:
        compact_direct(1)
        z_copy(TM2, UM2, last, 0, True)

    for u in range(tail):
        z_wait(TP2, u)
    pairs = ((TM1, TP2), (UM1, TP2), (TP2, TM1), (TP2, UM1), (TP2, TM2), (TP2, UM2))
    for a, (query, key) in enumerate(pairs):
        if key == UM2:
            for u in range(tail):
                z_wait(UM2, u)
        acc[a] = scores(query, key, 0, tail)

    def finish(a):
        query, key = pairs[a]
        return top(query, key, acc[a] + scores(query, key, tail, first[n]))

    by_z = range(tail, last if TM2 in direct else first[n])
    pass_on(by_z)
    for u in by_z:
        z_wait(TP2, u)
    send_part(PM1, jnp.maximum(early_m1, finish(0)), -1, False)
    send_part(PUM1, jnp.maximum(early_um1, finish(1)), -1, True)
    late = jnp.maximum(jnp.maximum(finish(2), finish(3)), finish(4))
    for u in range(tail, first[n]):
        z_wait(UM2, u)
    send_part(PP2, jnp.maximum(late, finish(5)), 2, False)

    arrived(part_recv, p_recv)
    mine = jnp.maximum(mine, jnp.max(part_recv[...].reshape(5, row_dev), axis=0, keepdims=True))
    back = dot_whole(jnp.where(from_src, mine, 0.0), home)
    ret_recv[0] = back[0:1]
    for k in range(1, shards):
        ret_send[k] = back[k : k + 1]
    for k in range(1, shards):
        remote(ret_send.at[k], ret_recv.at[k], r_send, r_recv, xy_dev(k, -1))
    arrived(ret_recv.at[pl.ds(1, shards - 1)], r_recv)
    out_ref[...] = jnp.sum(ret_recv[...].reshape(shards, row_dev), axis=0, keepdims=True)

    arrived(meta_send.at[pl.ds(1, shards - 1)], meta_ssem)
    for q in range(m):
        arrived(send_buf[q].at[pl.ds(1, shards - 1)], xy_send.at[q])
    for u in all_units:
        for b in range(1, 8):
            if u == last and (b in direct):
                continue
            arrived(blk.at[b, u], z_send.at[b, u])
    for b, _ in neighbours:
        arrived(raw.at[b], raw_ssem.at[b])
    if DIRECT:
        arrived(raw_target.at[pl.ds(1, len(direct))], rt_send)
    if DIRECT:
        arrived(counts.at[pl.ds(1, len(direct))], c_send)
    arrived(zmeta.at[pl.ds(1, 7)], zm_send)
    arrived(part_send, p_send)
    arrived(ret_send.at[pl.ds(1, shards - 1)], r_send)


def per_device(embedding, cluster_id, member_order):
    shards = lax.axis_size("shard")
    row_dev, depth = embedding.shape
    capacity = 5 * row_dev // (2 * shards)
    padded = -(-capacity // 16) * 16
    plan = PLAN
    n = len(plan)
    dma = pltpu.SemaphoreType.DMA
    vmem = pltpu.VMEM
    bf16, f32, i32 = jnp.bfloat16, jnp.float32, jnp.int32
    messages = [
        vmem((shards, padded if units == 1 else units * capacity, UNIT), bf16)
        for units in plan + (2,) * len(DIRECT)
    ]
    out = pl.pallas_call(
        functools.partial(kernel, shards, capacity, plan),
        out_shape=jax.ShapeDtypeStruct((1, row_dev), f32),
        in_specs=[pl.BlockSpec(memory_space=pltpu.HBM)] * 3,
        out_specs=pl.BlockSpec(memory_space=vmem),
        scratch_shapes=messages
        + messages
        + [
            vmem((row_dev, depth), bf16),
            vmem((1, row_dev), i32),
            vmem((1, row_dev), i32),
            vmem((8, depth // UNIT, row_dev, UNIT), bf16),
            vmem((6, row_dev, row_dev), f32),
            vmem((shards, 1, 128), f32),
            vmem((shards, 1, 128), f32),
            vmem((8, 1, row_dev), f32),
            vmem((5, row_dev, UNIT), bf16),
            vmem((5, 1, row_dev), f32),
            vmem((5, shards, 128), f32),
            vmem((8, row_dev, 128), f32),
            vmem((5, 1, row_dev), f32),
            vmem((5, 1, row_dev), f32),
            vmem((shards, 1, row_dev), f32),
            vmem((shards, 1, row_dev), f32),
            dma((3,)),
            dma((n + len(DIRECT),)),
            dma((n + len(DIRECT),)),
            dma,
            dma,
            dma((8, depth // UNIT)),
            dma((8, depth // UNIT)),
            dma,
            dma,
            dma((5,)),
            dma((5,)),
            dma,
            dma,
            dma,
            dma,
            dma,
            dma,
            dma,
            dma,
        ],
        compiler_params=pltpu.CompilerParams(
            collective_id=0, has_side_effects=True, vmem_limit_bytes=215 * 2**18
        ),
    )(embedding, cluster_id.reshape(1, row_dev), member_order.reshape(1, row_dev))
    return out.reshape(row_dev)


def solution(mesh):
    in_specs = (P(("shard", "grp"), None), P(("shard", "grp")), P(("shard", "grp")))
    out_specs = P(("shard", "grp"))
    return jax.shard_map(
        per_device, mesh=mesh, in_specs=in_specs, out_specs=out_specs, check_vma=False
    )
```

```python
import functools

import jax
import jax.numpy as jnp
from jax import lax
from jax.experimental import pallas as pl
from jax.experimental.pallas import tpu as pltpu
from jax.sharding import PartitionSpec as P

MESH = pl.DeviceIdType.MESH
HIGHEST = lax.Precision.HIGHEST
CLUST_OWN = 4
SIDE = 4
RANKS = 65536
UNIT = 128
PREPARE = 2
PLAN = (1, 1, 2, 2)

T0, TP1, TM1, TP2, TM2, U0, UM1, UM2 = range(8)
PP1, PU0 = range(2)
LATE = ((TM1, -1, False), (UM1, -1, True), (TP2, 2, False))
DIRECT = ((TM1, TP1), (TM2, TP2))


def iota(shape, dim):
    return lax.broadcasted_iota(jnp.int32, shape, dim)


def one_hot(cond, dtype=jnp.bfloat16):
    return jnp.where(cond, 1.0, 0.0).astype(dtype)


def dot_nt(a, b, precision=None):
    return lax.dot_general(
        a, b, (((1,), (1,)), ((), ())), preferred_element_type=jnp.float32, precision=precision
    )


def dot_nn(a, b, precision=None):
    return lax.dot_general(
        a, b, (((1,), (0,)), ((), ())), preferred_element_type=jnp.float32, precision=precision
    )


def dot_whole(a, selector):
    rows = a.shape[0]
    pieces = []
    for _ in range(3):
        pieces.append(a.astype(jnp.bfloat16))
        a = a - pieces[-1].astype(jnp.float32)
    out = dot_nt(jnp.concatenate(pieces, axis=0), selector)
    return out[:rows] + out[rows : 2 * rows] + out[2 * rows :]


def kernel(shards, capacity, plan, emb_hbm, cid_ref, rank_ref, out_ref, *refs):
    n = len(plan)
    m = n + len(DIRECT)
    send_buf, recv_buf, refs = refs[:m], refs[m : 2 * m], refs[2 * m :]
    (
        emb_ref,
        blk,
        acc,
        meta_send,
        meta_recv,
        zmeta,
        raw,
        raw_target,
        counts,
        kcol,
        part_send,
        part_recv,
        ret_send,
        ret_recv,
        in_sem,
        xy_send,
        xy_recv,
        meta_ssem,
        meta_rsem,
        z_send,
        z_recv,
        zm_send,
        zm_recv,
        raw_ssem,
        raw_rsem,
        rt_send,
        rt_recv,
        c_send,
        c_recv,
        p_send,
        p_recv,
        r_send,
        r_recv,
    ) = refs
    row_dev = emb_ref.shape[0]
    padded = -(-capacity // 16) * 16
    first = [sum(plan[:q]) for q in range(n + 1)]
    last = first[n] - 1 if DIRECT else first[n]
    direct = [b for pair in DIRECT for b in pair]
    me = lax.axis_index("shard")
    grp = lax.axis_index("grp")
    y, x = me // SIDE, me % SIDE
    z, core = grp // 2, grp % 2
    n_z = lax.axis_size("grp") // 2

    load = pltpu.make_async_copy(emb_hbm, emb_ref, in_sem)
    load.start()

    def xy_dev(k, sign):
        dy, dx = k // SIDE, k % SIDE
        py = (y + sign * dy + SIDE) % SIDE
        px = (x + sign * dx + SIDE) % SIDE
        return (py * SIDE + px, grp)

    def z_dev(dz, other):
        pc = 1 - core if other else core
        return (me, ((z + dz + n_z) % n_z) * 2 + pc)

    barrier = pltpu.get_barrier_semaphore()
    for k in range(1, shards):
        pl.semaphore_signal(barrier, inc=1, device_id=xy_dev(k, 1), device_id_type=MESH)
    column = [(d, o) for d in (-2, -1, 0, 1, 2) for o in (False, True) if (d, o) != (0, False)]
    for d, o in column:
        pl.semaphore_signal(barrier, inc=1, device_id=z_dev(d, o), device_id_type=MESH)

    def remote(src, dst, ssem, rsem, dev):
        copy = pltpu.make_async_remote_copy(
            src_ref=src, dst_ref=dst, send_sem=ssem, recv_sem=rsem, device_id=dev, device_id_type=MESH
        )
        copy.start()

    def arrived(ref, sem):
        pltpu.make_async_copy(ref, ref, sem).wait()

    cid = cid_ref[...]
    owner = cid // CLUST_OWN
    rel = ((owner // SIDE - y + SIDE) % SIDE) * SIDE + (owner % SIDE - x + SIDE) % SIDE
    is_owner = iota((shards, row_dev), 0) == rel
    earlier = one_hot(iota((row_dev, row_dev), 0) < iota((row_dev, row_dev), 1))
    before = dot_nn(one_hot(is_owner), earlier)
    slot = jnp.sum(jnp.where(is_owner, before, 0.0), axis=0, keepdims=True).astype(jnp.int32)
    target = rel * padded + slot
    pack = one_hot(iota((shards * padded, row_dev), 0) == target)

    key_own = (cid * RANKS + rank_ref[...] + 1).astype(jnp.float32)
    row_no = (iota((1, row_dev), 1) + 1).astype(jnp.float32)
    lane_k = iota((128, row_dev), 0)
    meta = dot_whole(jnp.where(is_owner, key_own, 0.0), one_hot(lane_k == slot)) + dot_nt(
        jnp.where(is_owner, row_no, 0.0).astype(jnp.bfloat16), one_hot(lane_k == slot + 64)
    )
    meta_recv[0] = meta[0:1]
    for k in range(1, shards):
        meta_send[k] = meta[k : k + 1]

    load.wait()
    wide = emb_ref[...].astype(jnp.float32)
    normed = (
        wide * lax.rsqrt(jnp.sum(wide * wide, axis=1, keepdims=True) + 1e-06)
    ).astype(jnp.bfloat16)

    if DIRECT:
        raw[T0] = normed[:, last * UNIT :]
        raw_target[T0] = target.astype(jnp.float32)
    neighbours = [bd for bd in ((TP1, -1), (TM1, 1), (TP2, -2), (TM2, 2)) if bd[0] in direct]

    def pack_chunk(q):
        rows = dot_nn(pack, normed[:, first[q] * UNIT : first[q + 1] * UNIT])
        rows = rows.reshape(shards, padded, plan[q] * UNIT)
        if plan[q] == 2:
            rows = jnp.concatenate(
                [rows[:, :capacity, :UNIT], rows[:, :capacity, UNIT:]], axis=1
            )
        rows = rows.astype(jnp.bfloat16)
        recv_buf[q][0] = rows[0]
        send_buf[q][1:] = rows[1:]

    def send_chunk(q):
        for k in range(1, shards):
            remote(
                send_buf[q].at[k], recv_buf[q].at[k], xy_send.at[q], xy_recv.at[q], xy_dev(k, 1)
            )

    pack_chunk(0)
    pl.semaphore_wait(barrier, shards - 1 + len(column))
    send_chunk(0)
    for k in range(1, shards):
        remote(meta_send.at[k], meta_recv.at[k], meta_ssem, meta_rsem, xy_dev(k, 1))
    for b, d in neighbours:
        remote(raw_target.at[T0], raw_target.at[b], rt_send, rt_recv, z_dev(d, False))
        remote(raw.at[T0], raw.at[b], raw_ssem.at[b], raw_rsem.at[b], z_dev(d, False))
    for q in range(1, n):
        pack_chunk(q)
        send_chunk(q)

    def pack_direct(e):
        halves = []
        for b in DIRECT[e]:
            arrived(raw.at[b], raw_rsem.at[b])
            to = raw_target[b].astype(jnp.int32)
            rows = dot_nn(one_hot(iota((shards * padded, row_dev), 0) == to), raw[b])
            halves.append(rows.reshape(shards, padded, UNIT)[:, :capacity])
        rows = jnp.concatenate(halves, axis=1).astype(jnp.bfloat16)
        recv_buf[n + e][0] = rows[0]
        send_buf[n + e][1:] = rows[1:]
        send_chunk(n + e)

    arrived(meta_recv.at[pl.ds(1, shards - 1)], meta_rsem)
    got = meta_recv[...].reshape(shards, 128)
    lanes = iota((shards, 128), 1)
    count = jnp.sum(jnp.where((got > 0.0) & (lanes < 64), 1.0, 0.0), axis=1, keepdims=True)
    lower = iota((shards, shards), 1) < iota((shards, shards), 0)
    count_row = jnp.sum(
        jnp.where(iota((shards, shards), 0) == iota((shards, shards), 1), count, 0.0),
        axis=0,
        keepdims=True,
    )
    offset = jnp.sum(jnp.where(lower, count_row, 0.0), axis=1, keepdims=True).astype(jnp.int32)
    count = count.astype(jnp.int32)

    def place(units, h, offset=offset, count=count):
        rows = padded if units == 1 else units * capacity
        k = iota((shards, shards * rows), 1) - iota((shards, shards * rows), 0) * rows - h * capacity
        good = (k >= 0) & (k < count)
        where_to = jnp.sum(jnp.where(good, offset + k + 1, 0), axis=0, keepdims=True) - 1
        return one_hot(iota((row_dev, shards * rows), 0) == where_to)

    gathers = {}

    def compact(q):
        units = plan[q]
        for h in range(units):
            if (units, h) not in gathers:
                gathers[units, h] = place(units, h)
        arrived(recv_buf[q].at[pl.ds(1, shards - 1)], xy_recv.at[q])
        rows = recv_buf[q][...]
        rows = rows.reshape(rows.shape[0] * rows.shape[1], UNIT)
        for h in range(units):
            blk[T0, first[q] + h] = dot_nn(gathers[units, h], rows).astype(jnp.bfloat16)
            send_own(first[q] + h)

    def direct_places(e):
        places = []
        for h, b in enumerate(DIRECT[e]):
            packed = counts[b][:, :1].astype(jnp.int32)
            places.append(place(2, h, packed % 1024, packed // 1024))
        return places

    def compact_direct(e):
        arrived(recv_buf[n + e].at[pl.ds(1, shards - 1)], xy_recv.at[n + e])
        rows = recv_buf[n + e][...]
        rows = rows.reshape(rows.shape[0] * rows.shape[1], UNIT)
        for h, b in enumerate(DIRECT[e]):
            blk[b, last] = dot_nn(direct_gather[e][h], rows).astype(jnp.bfloat16)
            if b == TM1:
                if TM2 not in direct:
                    z_copy(TM1, TM2, last, 1, False)
                z_copy(TM1, UM1, last, 0, True)
            elif b == TP1 and TP2 not in direct:
                z_copy(TP1, TP2, last, -1, False)
            elif b == TM2:
                z_copy(TM2, UM2, last, 0, True)

    def z_copy(src_slot, dst_slot, u, d, o):
        remote(
            blk.at[src_slot, u],
            blk.at[dst_slot, u],
            z_send.at[dst_slot, u],
            z_recv.at[dst_slot, u],
            z_dev(d, o),
        )

    def z_wait(slot_no, u):
        arrived(blk.at[slot_no, u], z_recv.at[slot_no, u])

    def units_of(q):
        return range(first[q], first[q + 1])

    def send_own(u):
        if u != last:
            z_copy(T0, TM1, u, 1, False)
            z_copy(T0, TP1, u, -1, False)
        z_copy(T0, U0, u, 0, True)

    def forward(q):
        for u in units_of(q):
            if u == last:
                continue
            z_wait(TM1, u)
            z_copy(TM1, TM2, u, 1, False)
            z_copy(TM1, UM1, u, 0, True)
            z_wait(TP1, u)
            z_copy(TP1, TP2, u, -1, False)

    compact(0)

    member = iota((shards, row_dev), 1)
    from_src = (member >= offset) & (member < offset + count)
    within = iota((1, row_dev), 1) - jnp.sum(jnp.where(from_src, offset, 0), axis=0, keepdims=True)
    got_t = jnp.concatenate([got, jnp.zeros((128 - shards, 128), jnp.float32)], axis=0).T
    from_pad = jnp.concatenate(
        [one_hot(from_src, jnp.float32), jnp.zeros((128 - shards, row_dev), jnp.float32)], axis=0
    )
    spread = dot_nn(got_t, from_pad, HIGHEST)
    key_row = jnp.sum(jnp.where(lane_k == within, spread, 0.0), axis=0, keepdims=True) - 1.0
    home_row = jnp.sum(jnp.where(lane_k == within + 64, spread, 0.0), axis=0, keepdims=True) - 1.0
    counts[T0] = jnp.broadcast_to((offset + 1024 * count).astype(jnp.float32), (shards, 128))
    for b, d in neighbours:
        remote(counts.at[T0], counts.at[b], c_send, c_recv, z_dev(d, False))
    source = jnp.sum(jnp.where(from_src, iota((shards, row_dev), 0), 0), axis=0, keepdims=True)
    zmeta[T0] = jnp.concatenate(
        [key_row, source.astype(jnp.float32) * row_dev + home_row], axis=0
    )
    for slot_no, d, o in (
        (TP1, -1, False),
        (TM1, 1, False),
        (TP2, -2, False),
        (TM2, 2, False),
        (U0, 0, True),
        (UM1, 1, True),
        (UM2, 2, True),
    ):
        remote(zmeta.at[T0], zmeta.at[slot_no], zm_send, zm_recv, z_dev(d, o))

    if DIRECT:
        arrived(raw_target.at[pl.ds(1, len(direct))], rt_recv)
    for q in range(1, n):
        compact(q)
        if q <= len(DIRECT):
            pack_direct(q - 1)
        forward(q - 1)
        if q == PREPARE:
            home = one_hot(iota((row_dev, row_dev), 0) == home_row.astype(jnp.int32))
            arrived(zmeta.at[pl.ds(1, 7)], zm_recv)
            keys = zmeta[:, 0, :]
            late_src, late_home = [], []
            for b, _, _ in LATE:
                code = zmeta[b, 1:2, :].astype(jnp.int32)
                late_src.append(iota((shards, row_dev), 0) == code // row_dev)
                late_home.append(one_hot(iota((row_dev, row_dev), 0) == code % row_dev))
            eye = one_hot(iota((row_dev, row_dev), 0) == iota((row_dev, row_dev), 1), jnp.float32)
            keys_t = dot_nt(eye, keys, HIGHEST)
            for b in range(8):
                kcol[b] = jnp.broadcast_to(keys_t[:, b : b + 1], (row_dev, 128))
            first_key = jnp.floor(keys * (1.0 / RANKS)) * RANKS
            if DIRECT:
                arrived(counts.at[pl.ds(1, len(direct))], c_recv)
            direct_gather = [direct_places(e) for e in range(len(DIRECT))]
    forward(n - 1)
    if DIRECT:
        compact_direct(0)

    def scores(query, key, start, stop):
        total = None
        for u in range(start, stop, 2):
            take = range(u, min(u + 2, stop))
            a = jnp.concatenate([blk[key, v] for v in take], axis=1)
            b = jnp.concatenate([blk[query, v] for v in take], axis=1)
            term = dot_nt(a, b)
            total = term if total is None else total + term
        return total

    def top(query, key, total):
        col = jnp.concatenate([kcol[key]] * (row_dev // 128), axis=1)
        allowed = (col < keys[query : query + 1]) & (col >= first_key[query : query + 1])
        return jnp.max(jnp.where(allowed, total, -1.0), axis=0, keepdims=True)

    def best(query, key_slots):
        running = None
        for key in key_slots:
            found = top(query, key, scores(query, key, 0, first[n]))
            running = found if running is None else jnp.maximum(running, found)
        return running

    def send_part(p, value, d, o):
        part_send[p] = value
        remote(part_send.at[p], part_recv.at[p], p_send, p_recv, z_dev(d, o))

    all_units = range(first[n])
    tail = first[n] - 2

    def pass_on(units):
        for u in units:
            z_wait(TM2, u)
            z_copy(TM2, UM2, u, 0, True)

    pass_on(range(first[n - 2]))
    for u in all_units:
        z_wait(U0, u)
    mine = best(T0, (T0, U0, TP1))
    send_part(PU0, best(U0, (TP1,)), 0, True)
    early_p1 = best(TP1, (T0, U0, TM1))
    early_m1 = best(TM1, (TP1,))
    for u in all_units:
        z_wait(UM1, u)
    send_part(PP1, jnp.maximum(early_p1, best(TP1, (UM1,))), 1, False)
    early_um1 = best(UM1, (TP1,))

    def give_back(group, value, chosen, rows, d, o):
        back = dot_whole(jnp.where(chosen, value, 0.0), rows)
        ret_send[group] = back.reshape(shards, 1, row_dev)
        for k in range(shards):
            if group == 0 and k == 0:
                continue
            plane, _ = xy_dev(k, -1)
            remote(
                ret_send.at[group, k],
                ret_recv.at[group, k],
                r_send.at[group],
                r_recv.at[group],
                (plane, z_dev(d, o)[1]),
            )
        if group == 0:
            ret_recv[0, 0] = back[0:1]

    def give_late(group, value):
        _, d, o = LATE[group - 1]
        give_back(group, value, late_src[group - 1], late_home[group - 1], d, o)
    pass_on(range(first[n - 2], tail))
    if len(DIRECT) > 1:
        compact_direct(1)

    for u in range(tail):
        z_wait(TP2, u)
    pairs = ((TM1, TP2), (UM1, TP2), (TP2, TM1), (TP2, UM1), (TP2, TM2), (TP2, UM2))
    for a, (query, key) in enumerate(pairs):
        if key == UM2:
            for u in range(tail):
                z_wait(UM2, u)
        acc[a] = scores(query, key, 0, tail)

    def finish(a):
        query, key = pairs[a]
        return top(query, key, acc[a] + scores(query, key, tail, first[n]))

    by_z = range(tail, last if TM2 in direct else first[n])
    pass_on(by_z)
    for u in by_z:
        z_wait(TP2, u)
    late_m1 = jnp.maximum(early_m1, finish(0))
    late_um1 = jnp.maximum(early_um1, finish(1))
    late = jnp.maximum(jnp.maximum(finish(2), finish(3)), finish(4))
    for u in range(tail, first[n]):
        z_wait(UM2, u)
    give_late(3, jnp.maximum(late, finish(5)))
    give_late(1, late_m1)
    give_late(2, late_um1)

    arrived(part_recv, p_recv)
    mine = jnp.maximum(mine, jnp.max(part_recv[...].reshape(2, row_dev), axis=0, keepdims=True))
    give_back(0, mine, from_src, home, 0, False)

    arrived(ret_recv.at[0, pl.ds(1, shards - 1)], r_recv.at[0])
    for group in range(1, 1 + len(LATE)):
        arrived(ret_recv.at[group], r_recv.at[group])
    found = jnp.sum(ret_recv[...].reshape(1 + len(LATE), shards, row_dev), axis=1)
    out_ref[...] = jnp.max(found, axis=0, keepdims=True)

    arrived(meta_send.at[pl.ds(1, shards - 1)], meta_ssem)
    for q in range(m):
        arrived(send_buf[q].at[pl.ds(1, shards - 1)], xy_send.at[q])
    for u in all_units:
        for b in range(1, 8):
            if u == last and (b in direct):
                continue
            arrived(blk.at[b, u], z_send.at[b, u])
    for b, _ in neighbours:
        arrived(raw.at[b], raw_ssem.at[b])
    if DIRECT:
        arrived(raw_target.at[pl.ds(1, len(direct))], rt_send)
    if DIRECT:
        arrived(counts.at[pl.ds(1, len(direct))], c_send)
    arrived(zmeta.at[pl.ds(1, 7)], zm_send)
    arrived(part_send, p_send)
    arrived(ret_send.at[0, pl.ds(1, shards - 1)], r_send.at[0])
    for group in range(1, 1 + len(LATE)):
        arrived(ret_send.at[group], r_send.at[group])


def per_device(embedding, cluster_id, member_order):
    shards = lax.axis_size("shard")
    row_dev, depth = embedding.shape
    capacity = 5 * row_dev // (2 * shards)
    padded = -(-capacity // 16) * 16
    plan = PLAN
    n = len(plan)
    dma = pltpu.SemaphoreType.DMA
    vmem = pltpu.VMEM
    bf16, f32 = jnp.bfloat16, jnp.float32
    messages = [
        vmem((shards, padded if units == 1 else units * capacity, UNIT), bf16)
        for units in plan + (2,) * len(DIRECT)
    ]
    out = pl.pallas_call(
        functools.partial(kernel, shards, capacity, plan),
        out_shape=jax.ShapeDtypeStruct((1, row_dev), f32),
        in_specs=[pl.BlockSpec(memory_space=pltpu.HBM)] + [pl.BlockSpec(memory_space=vmem)] * 2,
        out_specs=pl.BlockSpec(memory_space=vmem),
        scratch_shapes=messages
        + messages
        + [
            vmem((row_dev, depth), bf16),
            vmem((8, depth // UNIT, row_dev, UNIT), bf16),
            vmem((6, row_dev, row_dev), f32),
            vmem((shards, 1, 128), f32),
            vmem((shards, 1, 128), f32),
            vmem((8, 2, row_dev), f32),
            vmem((5, row_dev, UNIT), bf16),
            vmem((5, 1, row_dev), f32),
            vmem((5, shards, 128), f32),
            vmem((8, row_dev, 128), f32),
            vmem((2, 1, row_dev), f32),
            vmem((2, 1, row_dev), f32),
            vmem((1 + len(LATE), shards, 1, row_dev), f32),
            vmem((1 + len(LATE), shards, 1, row_dev), f32),
            dma,
            dma((n + len(DIRECT),)),
            dma((n + len(DIRECT),)),
            dma,
            dma,
            dma((8, depth // UNIT)),
            dma((8, depth // UNIT)),
            dma,
            dma,
            dma((5,)),
            dma((5,)),
            dma,
            dma,
            dma,
            dma,
            dma,
            dma,
            dma((1 + len(LATE),)),
            dma((1 + len(LATE),)),
        ],
        compiler_params=pltpu.CompilerParams(
            collective_id=0, has_side_effects=True, vmem_limit_bytes=215 * 2**18
        ),
    )(embedding, cluster_id.reshape(1, row_dev), member_order.reshape(1, row_dev))
    return out.reshape(row_dev)


def solution(mesh):
    in_specs = (P(("shard", "grp"), None), P(("shard", "grp")), P(("shard", "grp")))
    out_specs = P(("shard", "grp"))
    return jax.shard_map(
        per_device, mesh=mesh, in_specs=in_specs, out_specs=out_specs, check_vma=False
    )
```

```python
import functools

import jax
import jax.numpy as jnp
from jax import lax
from jax.experimental import pallas as pl
from jax.experimental.pallas import tpu as pltpu
from jax.sharding import PartitionSpec as P

MESH = pl.DeviceIdType.MESH
HIGHEST = lax.Precision.HIGHEST
CLUST_OWN = 4
SIDE = 4
RANKS = 65536
UNIT = 128
PREPARE = 2
PLAN = (1, 1, 2, 2)

T0, TP1, TM1, TP2, TM2, U0, UM1, UM2 = range(8)
PP1, PU0 = range(2)
LATE = ((TM1, -1, False), (UM1, -1, True), (TP2, 2, False))
DIRECT = ((TM1, TP1), (TM2, TP2))


def iota(shape, dim):
    return lax.broadcasted_iota(jnp.int32, shape, dim)


def one_hot(cond, dtype=jnp.bfloat16):
    return jnp.where(cond, 1.0, 0.0).astype(dtype)


def dot_nt(a, b, precision=None):
    return lax.dot_general(
        a, b, (((1,), (1,)), ((), ())), preferred_element_type=jnp.float32, precision=precision
    )


def dot_nn(a, b, precision=None):
    return lax.dot_general(
        a, b, (((1,), (0,)), ((), ())), preferred_element_type=jnp.float32, precision=precision
    )


def dot_whole(a, selector):
    rows = a.shape[0]
    pieces = []
    for _ in range(3):
        pieces.append(a.astype(jnp.bfloat16))
        a = a - pieces[-1].astype(jnp.float32)
    out = dot_nt(jnp.concatenate(pieces, axis=0), selector)
    return out[:rows] + out[rows : 2 * rows] + out[2 * rows :]


def kernel(shards, capacity, plan, emb_hbm, cid_ref, rank_ref, out_ref, *refs):
    n = len(plan)
    m = n + len(DIRECT)
    send_buf, recv_buf, refs = refs[:m], refs[m : 2 * m], refs[2 * m :]
    (
        emb_ref,
        blk,
        acc,
        meta_send,
        meta_recv,
        zmeta,
        raw,
        raw_target,
        counts,
        kcol,
        part_send,
        part_recv,
        ret_send,
        ret_recv,
        in_sem,
        xy_send,
        xy_recv,
        meta_ssem,
        meta_rsem,
        z_send,
        z_recv,
        zm_send,
        zm_recv,
        raw_ssem,
        raw_rsem,
        rt_send,
        rt_recv,
        c_send,
        c_recv,
        p_send,
        p_recv,
        r_send,
        r_recv,
    ) = refs
    row_dev = emb_ref.shape[0]
    padded = -(-capacity // 16) * 16
    first = [sum(plan[:q]) for q in range(n + 1)]
    last = first[n] - 1 if DIRECT else first[n]
    direct = [b for pair in DIRECT for b in pair]
    me = lax.axis_index("shard")
    grp = lax.axis_index("grp")
    y, x = me // SIDE, me % SIDE
    z, core = grp // 2, grp % 2
    n_z = lax.axis_size("grp") // 2

    load = pltpu.make_async_copy(emb_hbm, emb_ref, in_sem)
    load.start()

    def xy_dev(k, sign):
        dy, dx = k // SIDE, k % SIDE
        py = (y + sign * dy + SIDE) % SIDE
        px = (x + sign * dx + SIDE) % SIDE
        return (py * SIDE + px, grp)

    def z_dev(dz, other):
        pc = 1 - core if other else core
        return (me, ((z + dz + n_z) % n_z) * 2 + pc)

    barrier = pltpu.get_barrier_semaphore()
    for k in range(1, shards):
        pl.semaphore_signal(barrier, inc=1, device_id=xy_dev(k, 1), device_id_type=MESH)
    column = [(d, o) for d in (-2, -1, 0, 1, 2) for o in (False, True) if (d, o) != (0, False)]
    for d, o in column:
        pl.semaphore_signal(barrier, inc=1, device_id=z_dev(d, o), device_id_type=MESH)

    def remote(src, dst, ssem, rsem, dev):
        copy = pltpu.make_async_remote_copy(
            src_ref=src, dst_ref=dst, send_sem=ssem, recv_sem=rsem, device_id=dev, device_id_type=MESH
        )
        copy.start()

    def arrived(ref, sem):
        pltpu.make_async_copy(ref, ref, sem).wait()

    cid = cid_ref[...]
    owner = cid // CLUST_OWN
    rel = ((owner // SIDE - y + SIDE) % SIDE) * SIDE + (owner % SIDE - x + SIDE) % SIDE
    is_owner = iota((shards, row_dev), 0) == rel
    earlier = one_hot(iota((row_dev, row_dev), 0) < iota((row_dev, row_dev), 1))
    before = dot_nn(one_hot(is_owner), earlier)
    slot = jnp.sum(jnp.where(is_owner, before, 0.0), axis=0, keepdims=True).astype(jnp.int32)
    target = rel * padded + slot
    pack = one_hot(iota((shards * padded, row_dev), 0) == target)

    key_own = (cid * RANKS + rank_ref[...] + 1).astype(jnp.float32)
    row_no = (iota((1, row_dev), 1) + 1).astype(jnp.float32)
    lane_k = iota((128, row_dev), 0)
    meta = dot_whole(jnp.where(is_owner, key_own, 0.0), one_hot(lane_k == slot)) + dot_nt(
        jnp.where(is_owner, row_no, 0.0).astype(jnp.bfloat16), one_hot(lane_k == slot + 64)
    )
    meta_recv[0] = meta[0:1]
    for k in range(1, shards):
        meta_send[k] = meta[k : k + 1]

    load.wait()
    wide = emb_ref[...].astype(jnp.float32)
    normed = (
        wide * lax.rsqrt(jnp.sum(wide * wide, axis=1, keepdims=True) + 1e-06)
    ).astype(jnp.bfloat16)

    if DIRECT:
        raw[T0] = normed[:, last * UNIT :]
        raw_target[T0] = target.astype(jnp.float32)
    neighbours = [bd for bd in ((TP1, -1), (TM1, 1), (TP2, -2), (TM2, 2)) if bd[0] in direct]

    def pack_chunk(q):
        rows = dot_nn(pack, normed[:, first[q] * UNIT : first[q + 1] * UNIT])
        rows = rows.reshape(shards, padded, plan[q] * UNIT)
        if plan[q] == 2:
            rows = jnp.concatenate(
                [rows[:, :capacity, :UNIT], rows[:, :capacity, UNIT:]], axis=1
            )
        rows = rows.astype(jnp.bfloat16)
        recv_buf[q][0] = rows[0]
        send_buf[q][1:] = rows[1:]

    def send_chunk(q):
        for k in range(1, shards):
            remote(
                send_buf[q].at[k], recv_buf[q].at[k], xy_send.at[q], xy_recv.at[q], xy_dev(k, 1)
            )

    pack_chunk(0)
    pl.semaphore_wait(barrier, shards - 1 + len(column))
    send_chunk(0)
    for k in range(1, shards):
        remote(meta_send.at[k], meta_recv.at[k], meta_ssem, meta_rsem, xy_dev(k, 1))
    for b, d in neighbours:
        remote(raw_target.at[T0], raw_target.at[b], rt_send, rt_recv, z_dev(d, False))
        remote(raw.at[T0], raw.at[b], raw_ssem.at[b], raw_rsem.at[b], z_dev(d, False))
    for q in range(1, n):
        pack_chunk(q)
        send_chunk(q)

    def pack_direct(e):
        halves = []
        for b in DIRECT[e]:
            arrived(raw.at[b], raw_rsem.at[b])
            to = raw_target[b].astype(jnp.int32)
            rows = dot_nn(one_hot(iota((shards * padded, row_dev), 0) == to), raw[b])
            halves.append(rows.reshape(shards, padded, UNIT)[:, :capacity])
        rows = jnp.concatenate(halves, axis=1).astype(jnp.bfloat16)
        recv_buf[n + e][0] = rows[0]
        send_buf[n + e][1:] = rows[1:]
        send_chunk(n + e)

    arrived(meta_recv.at[pl.ds(1, shards - 1)], meta_rsem)
    got = meta_recv[...].reshape(shards, 128)
    lanes = iota((shards, 128), 1)
    count = jnp.sum(jnp.where((got > 0.0) & (lanes < 64), 1.0, 0.0), axis=1, keepdims=True)
    lower = iota((shards, shards), 1) < iota((shards, shards), 0)
    count_row = jnp.sum(
        jnp.where(iota((shards, shards), 0) == iota((shards, shards), 1), count, 0.0),
        axis=0,
        keepdims=True,
    )
    offset = jnp.sum(jnp.where(lower, count_row, 0.0), axis=1, keepdims=True).astype(jnp.int32)
    count = count.astype(jnp.int32)

    def place(units, h, offset=offset, count=count):
        rows = padded if units == 1 else units * capacity
        k = iota((shards, shards * rows), 1) - iota((shards, shards * rows), 0) * rows - h * capacity
        good = (k >= 0) & (k < count)
        where_to = jnp.sum(jnp.where(good, offset + k + 1, 0), axis=0, keepdims=True) - 1
        return one_hot(iota((row_dev, shards * rows), 0) == where_to)

    gathers = {}

    def compact(q):
        units = plan[q]
        for h in range(units):
            if (units, h) not in gathers:
                gathers[units, h] = place(units, h)
        arrived(recv_buf[q].at[pl.ds(1, shards - 1)], xy_recv.at[q])
        rows = recv_buf[q][...]
        rows = rows.reshape(rows.shape[0] * rows.shape[1], UNIT)
        for h in range(units):
            blk[T0, first[q] + h] = dot_nn(gathers[units, h], rows).astype(jnp.bfloat16)
            send_own(first[q] + h)

    def direct_places(e):
        places = []
        for h, b in enumerate(DIRECT[e]):
            packed = counts[b][:, :1].astype(jnp.int32)
            places.append(place(2, h, packed % 1024, packed // 1024))
        return places

    def compact_direct(e):
        arrived(recv_buf[n + e].at[pl.ds(1, shards - 1)], xy_recv.at[n + e])
        rows = recv_buf[n + e][...]
        rows = rows.reshape(rows.shape[0] * rows.shape[1], UNIT)
        for h, b in enumerate(DIRECT[e]):
            blk[b, last] = dot_nn(direct_gather[e][h], rows).astype(jnp.bfloat16)
            if b == TM1:
                if TM2 not in direct:
                    z_copy(TM1, TM2, last, 1, False)
                z_copy(TM1, UM1, last, 0, True)
            elif b == TP1 and TP2 not in direct:
                z_copy(TP1, TP2, last, -1, False)
            elif b == TM2:
                z_copy(TM2, UM2, last, 0, True)

    def z_copy(src_slot, dst_slot, u, d, o):
        remote(
            blk.at[src_slot, u],
            blk.at[dst_slot, u],
            z_send.at[dst_slot, u],
            z_recv.at[dst_slot, u],
            z_dev(d, o),
        )

    def z_wait(slot_no, u):
        arrived(blk.at[slot_no, u], z_recv.at[slot_no, u])

    def units_of(q):
        return range(first[q], first[q + 1])

    def send_own(u):
        if u != last:
            z_copy(T0, TM1, u, 1, False)
            z_copy(T0, TP1, u, -1, False)
        z_copy(T0, U0, u, 0, True)

    def forward(q):
        for u in units_of(q):
            if u == last:
                continue
            z_wait(TM1, u)
            z_copy(TM1, TM2, u, 1, False)
            z_copy(TM1, UM1, u, 0, True)
            z_wait(TP1, u)
            z_copy(TP1, TP2, u, -1, False)

    compact(0)

    member = iota((shards, row_dev), 1)
    from_src = (member >= offset) & (member < offset + count)
    within = iota((1, row_dev), 1) - jnp.sum(jnp.where(from_src, offset, 0), axis=0, keepdims=True)
    got_t = jnp.concatenate([got, jnp.zeros((128 - shards, 128), jnp.float32)], axis=0).T
    from_pad = jnp.concatenate(
        [one_hot(from_src, jnp.float32), jnp.zeros((128 - shards, row_dev), jnp.float32)], axis=0
    )
    spread = dot_nn(got_t, from_pad, HIGHEST)
    key_row = jnp.sum(jnp.where(lane_k == within, spread, 0.0), axis=0, keepdims=True) - 1.0
    home_row = jnp.sum(jnp.where(lane_k == within + 64, spread, 0.0), axis=0, keepdims=True) - 1.0
    counts[T0] = jnp.broadcast_to((offset + 1024 * count).astype(jnp.float32), (shards, 128))
    for b, d in neighbours:
        remote(counts.at[T0], counts.at[b], c_send, c_recv, z_dev(d, False))
    source = jnp.sum(jnp.where(from_src, iota((shards, row_dev), 0), 0), axis=0, keepdims=True)
    zmeta[T0] = jnp.concatenate(
        [key_row, source.astype(jnp.float32) * row_dev + home_row], axis=0
    )
    for slot_no, d, o in (
        (TP1, -1, False),
        (TM1, 1, False),
        (TP2, -2, False),
        (TM2, 2, False),
        (U0, 0, True),
        (UM1, 1, True),
        (UM2, 2, True),
    ):
        remote(zmeta.at[T0], zmeta.at[slot_no], zm_send, zm_recv, z_dev(d, o))

    if DIRECT:
        arrived(raw_target.at[pl.ds(1, len(direct))], rt_recv)
    for q in range(1, n):
        compact(q)
        if q <= len(DIRECT):
            pack_direct(q - 1)
        forward(q - 1)
        if q == PREPARE:
            home = one_hot(iota((row_dev, row_dev), 0) == home_row.astype(jnp.int32))
            arrived(zmeta.at[pl.ds(1, 7)], zm_recv)
            keys = zmeta[:, 0, :]
            late_src, late_home = [], []
            for b, _, _ in LATE:
                code = zmeta[b, 1:2, :].astype(jnp.int32)
                late_src.append(iota((shards, row_dev), 0) == code // row_dev)
                late_home.append(one_hot(iota((row_dev, row_dev), 0) == code % row_dev))
            eye = one_hot(iota((row_dev, row_dev), 0) == iota((row_dev, row_dev), 1), jnp.float32)
            keys_t = dot_nt(eye, keys, HIGHEST)
            for b in range(8):
                kcol[b] = jnp.broadcast_to(keys_t[:, b : b + 1], (row_dev, 128))
            first_key = jnp.floor(keys * (1.0 / RANKS)) * RANKS
            if DIRECT:
                arrived(counts.at[pl.ds(1, len(direct))], c_recv)
            direct_gather = [direct_places(e) for e in range(len(DIRECT))]
    if DIRECT:
        compact_direct(0)
    forward(n - 1)

    def scores(query, key, start, stop):
        total = None
        for u in range(start, stop, 2):
            take = range(u, min(u + 2, stop))
            a = jnp.concatenate([blk[key, v] for v in take], axis=1)
            b = jnp.concatenate([blk[query, v] for v in take], axis=1)
            term = dot_nt(a, b)
            total = term if total is None else total + term
        return total

    def top(query, key, total):
        col = jnp.concatenate([kcol[key]] * (row_dev // 128), axis=1)
        allowed = (col < keys[query : query + 1]) & (col >= first_key[query : query + 1])
        return jnp.max(jnp.where(allowed, total, -1.0), axis=0, keepdims=True)

    def best(query, key_slots):
        running = None
        for key in key_slots:
            found = top(query, key, scores(query, key, 0, first[n]))
            running = found if running is None else jnp.maximum(running, found)
        return running

    def send_part(p, value, d, o):
        part_send[p] = value
        remote(part_send.at[p], part_recv.at[p], p_send, p_recv, z_dev(d, o))

    all_units = range(first[n])
    tail = first[n] - 2

    def pass_on(units):
        for u in units:
            z_wait(TM2, u)
            z_copy(TM2, UM2, u, 0, True)

    pass_on(range(first[n - 2]))
    for u in all_units:
        z_wait(U0, u)
    mine = best(T0, (T0, U0, TP1))
    send_part(PU0, best(U0, (TP1,)), 0, True)
    early_p1 = best(TP1, (T0, U0, TM1))
    early_m1 = best(TM1, (TP1,))
    for u in all_units:
        z_wait(UM1, u)
    send_part(PP1, jnp.maximum(early_p1, best(TP1, (UM1,))), 1, False)
    early_um1 = best(UM1, (TP1,))

    def give_back(group, value, chosen, rows, d, o):
        back = dot_whole(jnp.where(chosen, value, 0.0), rows)
        ret_send[group] = back.reshape(shards, 1, row_dev)
        for k in range(shards):
            if group == 0 and k == 0:
                continue
            plane, _ = xy_dev(k, -1)
            remote(
                ret_send.at[group, k],
                ret_recv.at[group, k],
                r_send.at[group],
                r_recv.at[group],
                (plane, z_dev(d, o)[1]),
            )
        if group == 0:
            ret_recv[0, 0] = back[0:1]

    def give_late(group, value):
        _, d, o = LATE[group - 1]
        give_back(group, value, late_src[group - 1], late_home[group - 1], d, o)
    pass_on(range(first[n - 2], tail))
    if len(DIRECT) > 1:
        compact_direct(1)

    for u in range(tail):
        z_wait(TP2, u)
    pairs = ((TM1, TP2), (UM1, TP2), (TP2, TM1), (TP2, UM1), (TP2, TM2), (TP2, UM2))
    for a, (query, key) in enumerate(pairs):
        if key == UM2:
            for u in range(tail):
                z_wait(UM2, u)
        acc[a] = scores(query, key, 0, tail)

    def finish(a):
        query, key = pairs[a]
        return top(query, key, acc[a] + scores(query, key, tail, first[n]))

    by_z = range(tail, last if TM2 in direct else first[n])
    pass_on(by_z)
    for u in by_z:
        z_wait(TP2, u)
    late_m1 = jnp.maximum(early_m1, finish(0))
    late_um1 = jnp.maximum(early_um1, finish(1))
    late = jnp.maximum(jnp.maximum(finish(2), finish(3)), finish(4))
    for u in range(tail, first[n]):
        z_wait(UM2, u)
    give_late(3, jnp.maximum(late, finish(5)))
    give_late(1, late_m1)
    give_late(2, late_um1)

    arrived(part_recv, p_recv)
    mine = jnp.maximum(mine, jnp.max(part_recv[...].reshape(2, row_dev), axis=0, keepdims=True))
    give_back(0, mine, from_src, home, 0, False)

    arrived(ret_recv.at[0, pl.ds(1, shards - 1)], r_recv.at[0])
    for group in range(1, 1 + len(LATE)):
        arrived(ret_recv.at[group], r_recv.at[group])
    found = jnp.sum(ret_recv[...].reshape(1 + len(LATE), shards, row_dev), axis=1)
    out_ref[...] = jnp.max(found, axis=0, keepdims=True)

    arrived(meta_send.at[pl.ds(1, shards - 1)], meta_ssem)
    for q in range(m):
        arrived(send_buf[q].at[pl.ds(1, shards - 1)], xy_send.at[q])
    for u in all_units:
        for b in range(1, 8):
            if u == last and (b in direct):
                continue
            arrived(blk.at[b, u], z_send.at[b, u])
    for b, _ in neighbours:
        arrived(raw.at[b], raw_ssem.at[b])
    if DIRECT:
        arrived(raw_target.at[pl.ds(1, len(direct))], rt_send)
    if DIRECT:
        arrived(counts.at[pl.ds(1, len(direct))], c_send)
    arrived(zmeta.at[pl.ds(1, 7)], zm_send)
    arrived(part_send, p_send)
    arrived(ret_send.at[0, pl.ds(1, shards - 1)], r_send.at[0])
    for group in range(1, 1 + len(LATE)):
        arrived(ret_send.at[group], r_send.at[group])


def per_device(embedding, cluster_id, member_order):
    shards = lax.axis_size("shard")
    row_dev, depth = embedding.shape
    capacity = 5 * row_dev // (2 * shards)
    padded = -(-capacity // 16) * 16
    plan = PLAN
    n = len(plan)
    dma = pltpu.SemaphoreType.DMA
    vmem = pltpu.VMEM
    bf16, f32 = jnp.bfloat16, jnp.float32
    messages = [
        vmem((shards, padded if units == 1 else units * capacity, UNIT), bf16)
        for units in plan + (2,) * len(DIRECT)
    ]
    out = pl.pallas_call(
        functools.partial(kernel, shards, capacity, plan),
        out_shape=jax.ShapeDtypeStruct((1, row_dev), f32),
        in_specs=[pl.BlockSpec(memory_space=pltpu.HBM)] + [pl.BlockSpec(memory_space=vmem)] * 2,
        out_specs=pl.BlockSpec(memory_space=vmem),
        scratch_shapes=messages
        + messages
        + [
            vmem((row_dev, depth), bf16),
            vmem((8, depth // UNIT, row_dev, UNIT), bf16),
            vmem((6, row_dev, row_dev), f32),
            vmem((shards, 1, 128), f32),
            vmem((shards, 1, 128), f32),
            vmem((8, 2, row_dev), f32),
            vmem((5, row_dev, UNIT), bf16),
            vmem((5, 1, row_dev), f32),
            vmem((5, shards, 128), f32),
            vmem((8, row_dev, 128), f32),
            vmem((2, 1, row_dev), f32),
            vmem((2, 1, row_dev), f32),
            vmem((1 + len(LATE), shards, 1, row_dev), f32),
            vmem((1 + len(LATE), shards, 1, row_dev), f32),
            dma,
            dma((n + len(DIRECT),)),
            dma((n + len(DIRECT),)),
            dma,
            dma,
            dma((8, depth // UNIT)),
            dma((8, depth // UNIT)),
            dma,
            dma,
            dma((5,)),
            dma((5,)),
            dma,
            dma,
            dma,
            dma,
            dma,
            dma,
            dma((1 + len(LATE),)),
            dma((1 + len(LATE),)),
        ],
        compiler_params=pltpu.CompilerParams(
            collective_id=0, has_side_effects=True, vmem_limit_bytes=215 * 2**18
        ),
    )(embedding, cluster_id.reshape(1, row_dev), member_order.reshape(1, row_dev))
    return out.reshape(row_dev)


def solution(mesh):
    in_specs = (P(("shard", "grp"), None), P(("shard", "grp")), P(("shard", "grp")))
    out_specs = P(("shard", "grp"))
    return jax.shard_map(
        per_device, mesh=mesh, in_specs=in_specs, out_specs=out_specs, check_vma=False
    )
```

```python
import functools

import jax
import jax.numpy as jnp
from jax import lax
from jax.experimental import pallas as pl
from jax.experimental.pallas import tpu as pltpu
from jax.sharding import PartitionSpec as P

MESH = pl.DeviceIdType.MESH
HIGHEST = lax.Precision.HIGHEST
CLUST_OWN = 4
SIDE = 4
RANKS = 65536
UNIT = 128
PREPARE = 2
PLAN = (1, 1, 2, 2)

T0, TP1, TM1, TP2, TM2, U0, UM1, UM2 = range(8)
PP1, PU0 = range(2)
LATE = ((TM1, -1, False), (UM1, -1, True), (TP2, 2, False))
DIRECT = ((TM1, TP1), (TM2, TP2))


def iota(shape, dim):
    return lax.broadcasted_iota(jnp.int32, shape, dim)


def one_hot(cond, dtype=jnp.bfloat16):
    return jnp.where(cond, 1.0, 0.0).astype(dtype)


def dot_nt(a, b, precision=None):
    return lax.dot_general(
        a, b, (((1,), (1,)), ((), ())), preferred_element_type=jnp.float32, precision=precision
    )


def dot_nn(a, b, precision=None):
    return lax.dot_general(
        a, b, (((1,), (0,)), ((), ())), preferred_element_type=jnp.float32, precision=precision
    )


def dot_whole(a, selector):
    rows = a.shape[0]
    pieces = []
    for _ in range(3):
        pieces.append(a.astype(jnp.bfloat16))
        a = a - pieces[-1].astype(jnp.float32)
    out = dot_nt(jnp.concatenate(pieces, axis=0), selector)
    return out[:rows] + out[rows : 2 * rows] + out[2 * rows :]


def kernel(shards, capacity, plan, emb_hbm, cid_ref, rank_ref, out_ref, *refs):
    n = len(plan)
    m = n + len(DIRECT)
    send_buf, recv_buf, refs = refs[:m], refs[m : 2 * m], refs[2 * m :]
    (
        emb_ref,
        blk,
        acc,
        meta_send,
        meta_recv,
        zmeta,
        raw,
        raw_target,
        counts,
        kcol,
        part_send,
        part_recv,
        ret_send,
        ret_recv,
        in_sem,
        xy_send,
        xy_recv,
        meta_ssem,
        meta_rsem,
        z_send,
        z_recv,
        zm_send,
        zm_recv,
        raw_ssem,
        raw_rsem,
        rt_send,
        rt_recv,
        c_send,
        c_recv,
        p_send,
        p_recv,
        r_send,
        r_recv,
    ) = refs
    row_dev = emb_ref.shape[0]
    padded = -(-capacity // 16) * 16
    first = [sum(plan[:q]) for q in range(n + 1)]
    last = first[n] - 1 if DIRECT else first[n]
    direct = [b for pair in DIRECT for b in pair]
    me = lax.axis_index("shard")
    grp = lax.axis_index("grp")
    y, x = me // SIDE, me % SIDE
    z, core = grp // 2, grp % 2
    n_z = lax.axis_size("grp") // 2

    load = pltpu.make_async_copy(emb_hbm, emb_ref, in_sem)
    load.start()

    def xy_dev(k, sign):
        dy, dx = k // SIDE, k % SIDE
        py = (y + sign * dy + SIDE) % SIDE
        px = (x + sign * dx + SIDE) % SIDE
        return (py * SIDE + px, grp)

    def z_dev(dz, other):
        pc = 1 - core if other else core
        return (me, ((z + dz + n_z) % n_z) * 2 + pc)

    barrier = pltpu.get_barrier_semaphore()
    for k in range(1, shards):
        pl.semaphore_signal(barrier, inc=1, device_id=xy_dev(k, 1), device_id_type=MESH)
    column = [(d, o) for d in (-2, -1, 0, 1, 2) for o in (False, True) if (d, o) != (0, False)]
    for d, o in column:
        pl.semaphore_signal(barrier, inc=1, device_id=z_dev(d, o), device_id_type=MESH)

    def remote(src, dst, ssem, rsem, dev):
        copy = pltpu.make_async_remote_copy(
            src_ref=src, dst_ref=dst, send_sem=ssem, recv_sem=rsem, device_id=dev, device_id_type=MESH
        )
        copy.start()

    def arrived(ref, sem):
        pltpu.make_async_copy(ref, ref, sem).wait()

    cid = cid_ref[...]
    owner = cid // CLUST_OWN
    rel = ((owner // SIDE - y + SIDE) % SIDE) * SIDE + (owner % SIDE - x + SIDE) % SIDE
    is_owner = iota((shards, row_dev), 0) == rel
    earlier = one_hot(iota((row_dev, row_dev), 0) < iota((row_dev, row_dev), 1))
    before = dot_nn(one_hot(is_owner), earlier)
    slot = jnp.sum(jnp.where(is_owner, before, 0.0), axis=0, keepdims=True).astype(jnp.int32)
    target = rel * padded + slot
    pack = one_hot(iota((shards * padded, row_dev), 0) == target)

    key_own = (cid * RANKS + rank_ref[...] + 1).astype(jnp.float32)
    row_no = (iota((1, row_dev), 1) + 1).astype(jnp.float32)
    lane_k = iota((128, row_dev), 0)
    meta = dot_whole(jnp.where(is_owner, key_own, 0.0), one_hot(lane_k == slot)) + dot_nt(
        jnp.where(is_owner, row_no, 0.0).astype(jnp.bfloat16), one_hot(lane_k == slot + 64)
    )
    meta_recv[0] = meta[0:1]
    for k in range(1, shards):
        meta_send[k] = meta[k : k + 1]

    load.wait()
    wide = emb_ref[...].astype(jnp.float32)
    normed = (
        wide * lax.rsqrt(jnp.sum(wide * wide, axis=1, keepdims=True) + 1e-06)
    ).astype(jnp.bfloat16)

    if DIRECT:
        raw[T0] = normed[:, last * UNIT :]
        raw_target[T0] = target.astype(jnp.float32)
    neighbours = [bd for bd in ((TP1, -1), (TM1, 1), (TP2, -2), (TM2, 2)) if bd[0] in direct]

    def pack_chunk(q):
        rows = dot_nn(pack, normed[:, first[q] * UNIT : first[q + 1] * UNIT])
        rows = rows.reshape(shards, padded, plan[q] * UNIT)
        if plan[q] == 2:
            rows = jnp.concatenate(
                [rows[:, :capacity, :UNIT], rows[:, :capacity, UNIT:]], axis=1
            )
        rows = rows.astype(jnp.bfloat16)
        recv_buf[q][0] = rows[0]
        send_buf[q][1:] = rows[1:]

    def hops(k):
        dy, dx = k // SIDE, k % SIDE
        return min(dy, SIDE - dy) + min(dx, SIDE - dx)

    def send_chunk(q):
        for k in sorted(range(1, shards), key=hops, reverse=True):
            remote(
                send_buf[q].at[k], recv_buf[q].at[k], xy_send.at[q], xy_recv.at[q], xy_dev(k, 1)
            )

    pack_chunk(0)
    pl.semaphore_wait(barrier, shards - 1 + len(column))
    send_chunk(0)
    for k in range(1, shards):
        remote(meta_send.at[k], meta_recv.at[k], meta_ssem, meta_rsem, xy_dev(k, 1))
    for b, d in neighbours:
        remote(raw_target.at[T0], raw_target.at[b], rt_send, rt_recv, z_dev(d, False))
        remote(raw.at[T0], raw.at[b], raw_ssem.at[b], raw_rsem.at[b], z_dev(d, False))
    for q in range(1, n):
        pack_chunk(q)
        send_chunk(q)

    def pack_direct(e):
        halves = []
        for b in DIRECT[e]:
            arrived(raw.at[b], raw_rsem.at[b])
            to = raw_target[b].astype(jnp.int32)
            rows = dot_nn(one_hot(iota((shards * padded, row_dev), 0) == to), raw[b])
            halves.append(rows.reshape(shards, padded, UNIT)[:, :capacity])
        rows = jnp.concatenate(halves, axis=1).astype(jnp.bfloat16)
        recv_buf[n + e][0] = rows[0]
        send_buf[n + e][1:] = rows[1:]
        send_chunk(n + e)

    arrived(meta_recv.at[pl.ds(1, shards - 1)], meta_rsem)
    got = meta_recv[...].reshape(shards, 128)
    lanes = iota((shards, 128), 1)
    count = jnp.sum(jnp.where((got > 0.0) & (lanes < 64), 1.0, 0.0), axis=1, keepdims=True)
    lower = iota((shards, shards), 1) < iota((shards, shards), 0)
    count_row = jnp.sum(
        jnp.where(iota((shards, shards), 0) == iota((shards, shards), 1), count, 0.0),
        axis=0,
        keepdims=True,
    )
    offset = jnp.sum(jnp.where(lower, count_row, 0.0), axis=1, keepdims=True).astype(jnp.int32)
    count = count.astype(jnp.int32)

    def place(units, h, offset=offset, count=count):
        rows = padded if units == 1 else units * capacity
        k = iota((shards, shards * rows), 1) - iota((shards, shards * rows), 0) * rows - h * capacity
        good = (k >= 0) & (k < count)
        where_to = jnp.sum(jnp.where(good, offset + k + 1, 0), axis=0, keepdims=True) - 1
        return one_hot(iota((row_dev, shards * rows), 0) == where_to)

    gathers = {}

    def compact(q):
        units = plan[q]
        for h in range(units):
            if (units, h) not in gathers:
                gathers[units, h] = place(units, h)
        arrived(recv_buf[q].at[pl.ds(1, shards - 1)], xy_recv.at[q])
        rows = recv_buf[q][...]
        rows = rows.reshape(rows.shape[0] * rows.shape[1], UNIT)
        for h in range(units):
            blk[T0, first[q] + h] = dot_nn(gathers[units, h], rows).astype(jnp.bfloat16)
            send_own(first[q] + h)

    def direct_places(e):
        places = []
        for h, b in enumerate(DIRECT[e]):
            packed = counts[b][:, :1].astype(jnp.int32)
            places.append(place(2, h, packed % 1024, packed // 1024))
        return places

    def compact_direct(e):
        arrived(recv_buf[n + e].at[pl.ds(1, shards - 1)], xy_recv.at[n + e])
        rows = recv_buf[n + e][...]
        rows = rows.reshape(rows.shape[0] * rows.shape[1], UNIT)
        for h, b in enumerate(DIRECT[e]):
            blk[b, last] = dot_nn(direct_gather[e][h], rows).astype(jnp.bfloat16)
            if b == TM1:
                if TM2 not in direct:
                    z_copy(TM1, TM2, last, 1, False)
                z_copy(TM1, UM1, last, 0, True)
            elif b == TP1 and TP2 not in direct:
                z_copy(TP1, TP2, last, -1, False)
            elif b == TM2:
                z_copy(TM2, UM2, last, 0, True)

    def z_copy(src_slot, dst_slot, u, d, o):
        remote(
            blk.at[src_slot, u],
            blk.at[dst_slot, u],
            z_send.at[dst_slot, u],
            z_recv.at[dst_slot, u],
            z_dev(d, o),
        )

    def z_wait(slot_no, u):
        arrived(blk.at[slot_no, u], z_recv.at[slot_no, u])

    def units_of(q):
        return range(first[q], first[q + 1])

    def send_own(u):
        if u != last:
            z_copy(T0, TM1, u, 1, False)
            z_copy(T0, TP1, u, -1, False)
        z_copy(T0, U0, u, 0, True)

    def forward(q):
        for u in units_of(q):
            if u == last:
                continue
            z_wait(TM1, u)
            z_copy(TM1, TM2, u, 1, False)
            z_copy(TM1, UM1, u, 0, True)
            z_wait(TP1, u)
            z_copy(TP1, TP2, u, -1, False)

    compact(0)

    member = iota((shards, row_dev), 1)
    from_src = (member >= offset) & (member < offset + count)
    within = iota((1, row_dev), 1) - jnp.sum(jnp.where(from_src, offset, 0), axis=0, keepdims=True)
    got_t = jnp.concatenate([got, jnp.zeros((128 - shards, 128), jnp.float32)], axis=0).T
    from_pad = jnp.concatenate(
        [one_hot(from_src, jnp.float32), jnp.zeros((128 - shards, row_dev), jnp.float32)], axis=0
    )
    spread = dot_nn(got_t, from_pad, HIGHEST)
    key_row = jnp.sum(jnp.where(lane_k == within, spread, 0.0), axis=0, keepdims=True) - 1.0
    home_row = jnp.sum(jnp.where(lane_k == within + 64, spread, 0.0), axis=0, keepdims=True) - 1.0
    counts[T0] = jnp.broadcast_to((offset + 1024 * count).astype(jnp.float32), (shards, 128))
    for b, d in neighbours:
        remote(counts.at[T0], counts.at[b], c_send, c_recv, z_dev(d, False))
    source = jnp.sum(jnp.where(from_src, iota((shards, row_dev), 0), 0), axis=0, keepdims=True)
    zmeta[T0] = jnp.concatenate(
        [key_row, source.astype(jnp.float32) * row_dev + home_row], axis=0
    )
    for slot_no, d, o in (
        (TP1, -1, False),
        (TM1, 1, False),
        (TP2, -2, False),
        (TM2, 2, False),
        (U0, 0, True),
        (UM1, 1, True),
        (UM2, 2, True),
    ):
        remote(zmeta.at[T0], zmeta.at[slot_no], zm_send, zm_recv, z_dev(d, o))

    if DIRECT:
        arrived(raw_target.at[pl.ds(1, len(direct))], rt_recv)
    for q in range(1, n):
        compact(q)
        if q <= len(DIRECT):
            pack_direct(q - 1)
        forward(q - 1)
        if q == PREPARE:
            home = one_hot(iota((row_dev, row_dev), 0) == home_row.astype(jnp.int32))
            arrived(zmeta.at[pl.ds(1, 7)], zm_recv)
            keys = zmeta[:, 0, :]
            late_src, late_home = [], []
            for b, _, _ in LATE:
                code = zmeta[b, 1:2, :].astype(jnp.int32)
                late_src.append(iota((shards, row_dev), 0) == code // row_dev)
                late_home.append(one_hot(iota((row_dev, row_dev), 0) == code % row_dev))
            eye = one_hot(iota((row_dev, row_dev), 0) == iota((row_dev, row_dev), 1), jnp.float32)
            keys_t = dot_nt(eye, keys, HIGHEST)
            for b in range(8):
                kcol[b] = jnp.broadcast_to(keys_t[:, b : b + 1], (row_dev, 128))
            first_key = jnp.floor(keys * (1.0 / RANKS)) * RANKS
            if DIRECT:
                arrived(counts.at[pl.ds(1, len(direct))], c_recv)
            direct_gather = [direct_places(e) for e in range(len(DIRECT))]
    if DIRECT:
        compact_direct(0)
    forward(n - 1)

    def scores(query, key, start, stop):
        total = None
        for u in range(start, stop, 2):
            take = range(u, min(u + 2, stop))
            a = jnp.concatenate([blk[key, v] for v in take], axis=1)
            b = jnp.concatenate([blk[query, v] for v in take], axis=1)
            term = dot_nt(a, b)
            total = term if total is None else total + term
        return total

    def top(query, key, total):
        col = jnp.concatenate([kcol[key]] * (row_dev // 128), axis=1)
        allowed = (col < keys[query : query + 1]) & (col >= first_key[query : query + 1])
        return jnp.max(jnp.where(allowed, total, -1.0), axis=0, keepdims=True)

    def best(query, key_slots):
        running = None
        for key in key_slots:
            found = top(query, key, scores(query, key, 0, first[n]))
            running = found if running is None else jnp.maximum(running, found)
        return running

    def send_part(p, value, d, o):
        part_send[p] = value
        remote(part_send.at[p], part_recv.at[p], p_send, p_recv, z_dev(d, o))

    all_units = range(first[n])
    tail = first[n] - 2

    def pass_on(units):
        for u in units:
            z_wait(TM2, u)
            z_copy(TM2, UM2, u, 0, True)

    pass_on(range(first[n - 2]))
    for u in all_units:
        z_wait(U0, u)
    mine = best(T0, (T0, U0, TP1))
    send_part(PU0, best(U0, (TP1,)), 0, True)
    early_p1 = best(TP1, (T0, U0, TM1))
    early_m1 = best(TM1, (TP1,))
    for u in all_units:
        z_wait(UM1, u)
    send_part(PP1, jnp.maximum(early_p1, best(TP1, (UM1,))), 1, False)
    early_um1 = best(UM1, (TP1,))

    def give_back(group, value, chosen, rows, d, o):
        back = dot_whole(jnp.where(chosen, value, 0.0), rows)
        ret_send[group] = back.reshape(shards, 1, row_dev)
        for k in sorted(range(shards), key=hops, reverse=True):
            if group == 0 and k == 0:
                continue
            plane, _ = xy_dev(k, -1)
            remote(
                ret_send.at[group, k],
                ret_recv.at[group, k],
                r_send.at[group],
                r_recv.at[group],
                (plane, z_dev(d, o)[1]),
            )
        if group == 0:
            ret_recv[0, 0] = back[0:1]

    def give_late(group, value):
        _, d, o = LATE[group - 1]
        give_back(group, value, late_src[group - 1], late_home[group - 1], d, o)
    pass_on(range(first[n - 2], tail))
    if len(DIRECT) > 1:
        compact_direct(1)

    for u in range(tail):
        z_wait(TP2, u)
    pairs = ((TM1, TP2), (UM1, TP2), (TP2, TM1), (TP2, UM1), (TP2, TM2), (TP2, UM2))
    for a, (query, key) in enumerate(pairs):
        if key == UM2:
            for u in range(tail):
                z_wait(UM2, u)
        acc[a] = scores(query, key, 0, tail)

    def finish(a):
        query, key = pairs[a]
        return top(query, key, acc[a] + scores(query, key, tail, first[n]))

    by_z = range(tail, last if TM2 in direct else first[n])
    pass_on(by_z)
    for u in by_z:
        z_wait(TP2, u)
    late_m1 = jnp.maximum(early_m1, finish(0))
    late_um1 = jnp.maximum(early_um1, finish(1))
    late = jnp.maximum(jnp.maximum(finish(2), finish(3)), finish(4))
    for u in range(tail, first[n]):
        z_wait(UM2, u)
    give_late(3, jnp.maximum(late, finish(5)))
    give_late(1, late_m1)
    give_late(2, late_um1)

    arrived(part_recv, p_recv)
    mine = jnp.maximum(mine, jnp.max(part_recv[...].reshape(2, row_dev), axis=0, keepdims=True))
    give_back(0, mine, from_src, home, 0, False)

    arrived(ret_recv.at[0, pl.ds(1, shards - 1)], r_recv.at[0])
    for group in range(1, 1 + len(LATE)):
        arrived(ret_recv.at[group], r_recv.at[group])
    found = jnp.sum(ret_recv[...].reshape(1 + len(LATE), shards, row_dev), axis=1)
    out_ref[...] = jnp.max(found, axis=0, keepdims=True)

    arrived(meta_send.at[pl.ds(1, shards - 1)], meta_ssem)
    for q in range(m):
        arrived(send_buf[q].at[pl.ds(1, shards - 1)], xy_send.at[q])
    for u in all_units:
        for b in range(1, 8):
            if u == last and (b in direct):
                continue
            arrived(blk.at[b, u], z_send.at[b, u])
    for b, _ in neighbours:
        arrived(raw.at[b], raw_ssem.at[b])
    if DIRECT:
        arrived(raw_target.at[pl.ds(1, len(direct))], rt_send)
    if DIRECT:
        arrived(counts.at[pl.ds(1, len(direct))], c_send)
    arrived(zmeta.at[pl.ds(1, 7)], zm_send)
    arrived(part_send, p_send)
    arrived(ret_send.at[0, pl.ds(1, shards - 1)], r_send.at[0])
    for group in range(1, 1 + len(LATE)):
        arrived(ret_send.at[group], r_send.at[group])


def per_device(embedding, cluster_id, member_order):
    shards = lax.axis_size("shard")
    row_dev, depth = embedding.shape
    capacity = 5 * row_dev // (2 * shards)
    padded = -(-capacity // 16) * 16
    plan = PLAN
    n = len(plan)
    dma = pltpu.SemaphoreType.DMA
    vmem = pltpu.VMEM
    bf16, f32 = jnp.bfloat16, jnp.float32
    messages = [
        vmem((shards, padded if units == 1 else units * capacity, UNIT), bf16)
        for units in plan + (2,) * len(DIRECT)
    ]
    out = pl.pallas_call(
        functools.partial(kernel, shards, capacity, plan),
        out_shape=jax.ShapeDtypeStruct((1, row_dev), f32),
        in_specs=[pl.BlockSpec(memory_space=pltpu.HBM)] + [pl.BlockSpec(memory_space=vmem)] * 2,
        out_specs=pl.BlockSpec(memory_space=vmem),
        scratch_shapes=messages
        + messages
        + [
            vmem((row_dev, depth), bf16),
            vmem((8, depth // UNIT, row_dev, UNIT), bf16),
            vmem((6, row_dev, row_dev), f32),
            vmem((shards, 1, 128), f32),
            vmem((shards, 1, 128), f32),
            vmem((8, 2, row_dev), f32),
            vmem((5, row_dev, UNIT), bf16),
            vmem((5, 1, row_dev), f32),
            vmem((5, shards, 128), f32),
            vmem((8, row_dev, 128), f32),
            vmem((2, 1, row_dev), f32),
            vmem((2, 1, row_dev), f32),
            vmem((1 + len(LATE), shards, 1, row_dev), f32),
            vmem((1 + len(LATE), shards, 1, row_dev), f32),
            dma,
            dma((n + len(DIRECT),)),
            dma((n + len(DIRECT),)),
            dma,
            dma,
            dma((8, depth // UNIT)),
            dma((8, depth // UNIT)),
            dma,
            dma,
            dma((5,)),
            dma((5,)),
            dma,
            dma,
            dma,
            dma,
            dma,
            dma,
            dma((1 + len(LATE),)),
            dma((1 + len(LATE),)),
        ],
        compiler_params=pltpu.CompilerParams(
            collective_id=0, has_side_effects=True, vmem_limit_bytes=215 * 2**18
        ),
    )(embedding, cluster_id.reshape(1, row_dev), member_order.reshape(1, row_dev))
    return out.reshape(row_dev)


def solution(mesh):
    in_specs = (P(("shard", "grp"), None), P(("shard", "grp")), P(("shard", "grp")))
    out_specs = P(("shard", "grp"))
    return jax.shard_map(
        per_device, mesh=mesh, in_specs=in_specs, out_specs=out_specs, check_vma=False
    )
```

```python
import functools

import jax
import jax.numpy as jnp
from jax import lax
from jax.experimental import pallas as pl
from jax.experimental.pallas import tpu as pltpu
from jax.sharding import PartitionSpec as P

MESH = pl.DeviceIdType.MESH
HIGHEST = lax.Precision.HIGHEST
CLUST_OWN = 4
SIDE = 4
RANKS = 65536
UNIT = 128
PREPARE = 2
PLAN = (1, 1, 2, 2)

T0, TP1, TM1, TP2, TM2, U0, UM1, UM2 = range(8)
PP1, PU0 = range(2)
LATE = ((TM1, -1, False), (UM1, -1, True), (TP2, 2, False))
DIRECT = ((TM1, TP1), (TM2, TP2))


def iota(shape, dim):
    return lax.broadcasted_iota(jnp.int32, shape, dim)


def one_hot(cond, dtype=jnp.bfloat16):
    return jnp.where(cond, 1.0, 0.0).astype(dtype)


def dot_nt(a, b, precision=None):
    return lax.dot_general(
        a, b, (((1,), (1,)), ((), ())), preferred_element_type=jnp.float32, precision=precision
    )


def dot_nn(a, b, precision=None):
    return lax.dot_general(
        a, b, (((1,), (0,)), ((), ())), preferred_element_type=jnp.float32, precision=precision
    )


def dot_whole(a, selector):
    rows = a.shape[0]
    pieces = []
    for _ in range(3):
        pieces.append(a.astype(jnp.bfloat16))
        a = a - pieces[-1].astype(jnp.float32)
    out = dot_nt(jnp.concatenate(pieces, axis=0), selector)
    return out[:rows] + out[rows : 2 * rows] + out[2 * rows :]


def kernel(shards, capacity, plan, emb_hbm, cid_ref, rank_ref, out_ref, *refs):
    n = len(plan)
    m = n + len(DIRECT)
    send_buf, recv_buf, refs = refs[:m], refs[m : 2 * m], refs[2 * m :]
    (
        emb_ref,
        blk,
        acc,
        meta_send,
        meta_recv,
        zmeta,
        raw,
        raw_target,
        counts,
        kcol,
        part_send,
        part_recv,
        ret_send,
        ret_recv,
        in_sem,
        xy_send,
        xy_recv,
        meta_ssem,
        meta_rsem,
        z_send,
        z_recv,
        zm_send,
        zm_recv,
        raw_ssem,
        raw_rsem,
        rt_send,
        rt_recv,
        c_send,
        c_recv,
        p_send,
        p_recv,
        r_send,
        r_recv,
    ) = refs
    row_dev = emb_ref.shape[0]
    padded = -(-capacity // 16) * 16
    first = [sum(plan[:q]) for q in range(n + 1)]
    last = first[n] - 1 if DIRECT else first[n]
    direct = [b for pair in DIRECT for b in pair]
    me = lax.axis_index("shard")
    grp = lax.axis_index("grp")
    y, x = me // SIDE, me % SIDE
    z, core = grp // 2, grp % 2
    n_z = lax.axis_size("grp") // 2

    load = pltpu.make_async_copy(emb_hbm, emb_ref, in_sem)
    load.start()

    def xy_dev(k, sign):
        dy, dx = k // SIDE, k % SIDE
        py = (y + sign * dy + SIDE) % SIDE
        px = (x + sign * dx + SIDE) % SIDE
        return (py * SIDE + px, grp)

    def z_dev(dz, other):
        pc = 1 - core if other else core
        return (me, ((z + dz + n_z) % n_z) * 2 + pc)

    barrier = pltpu.get_barrier_semaphore()
    for k in range(1, shards):
        pl.semaphore_signal(barrier, inc=1, device_id=xy_dev(k, 1), device_id_type=MESH)
    column = [(d, o) for d in (-2, -1, 0, 1, 2) for o in (False, True) if (d, o) != (0, False)]
    for d, o in column:
        pl.semaphore_signal(barrier, inc=1, device_id=z_dev(d, o), device_id_type=MESH)

    def remote(src, dst, ssem, rsem, dev):
        copy = pltpu.make_async_remote_copy(
            src_ref=src, dst_ref=dst, send_sem=ssem, recv_sem=rsem, device_id=dev, device_id_type=MESH
        )
        copy.start()

    def arrived(ref, sem):
        pltpu.make_async_copy(ref, ref, sem).wait()

    cid = cid_ref[...]
    owner = cid // CLUST_OWN
    rel = ((owner // SIDE - y + SIDE) % SIDE) * SIDE + (owner % SIDE - x + SIDE) % SIDE
    is_owner = iota((shards, row_dev), 0) == rel
    earlier = one_hot(iota((row_dev, row_dev), 0) < iota((row_dev, row_dev), 1))
    before = dot_nn(one_hot(is_owner), earlier)
    slot = jnp.sum(jnp.where(is_owner, before, 0.0), axis=0, keepdims=True).astype(jnp.int32)
    target = rel * padded + slot
    pack = one_hot(iota((shards * padded, row_dev), 0) == target)

    key_own = (cid * RANKS + rank_ref[...] + 1).astype(jnp.float32)
    row_no = (iota((1, row_dev), 1) + 1).astype(jnp.float32)
    lane_k = iota((128, row_dev), 0)
    meta = dot_whole(jnp.where(is_owner, key_own, 0.0), one_hot(lane_k == slot)) + dot_nt(
        jnp.where(is_owner, row_no, 0.0).astype(jnp.bfloat16), one_hot(lane_k == slot + 64)
    )
    meta_recv[0] = meta[0:1]
    for k in range(1, shards):
        meta_send[k] = meta[k : k + 1]

    load.wait()
    wide = emb_ref[...].astype(jnp.float32)
    normed = (
        wide * lax.rsqrt(jnp.sum(wide * wide, axis=1, keepdims=True) + 1e-06)
    ).astype(jnp.bfloat16)

    if DIRECT:
        raw[T0] = normed[:, last * UNIT :]
        raw_target[T0] = target.astype(jnp.float32)
    neighbours = [bd for bd in ((TP1, -1), (TM1, 1), (TP2, -2), (TM2, 2)) if bd[0] in direct]

    def pack_chunk(q):
        rows = dot_nn(pack, normed[:, first[q] * UNIT : first[q + 1] * UNIT])
        rows = rows.reshape(shards, padded, plan[q] * UNIT)
        if plan[q] == 2:
            rows = jnp.concatenate(
                [rows[:, :capacity, :UNIT], rows[:, :capacity, UNIT:]], axis=1
            )
        rows = rows.astype(jnp.bfloat16)
        recv_buf[q][0] = rows[0]
        send_buf[q][1:] = rows[1:]

    def send_chunk(q):
        for k in range(1, shards):
            remote(
                send_buf[q].at[k], recv_buf[q].at[k], xy_send.at[q], xy_recv.at[q], xy_dev(k, 1)
            )

    pack_chunk(0)
    pl.semaphore_wait(barrier, shards - 1 + len(column))
    send_chunk(0)
    for k in range(1, shards):
        remote(meta_send.at[k], meta_recv.at[k], meta_ssem, meta_rsem, xy_dev(k, 1))
    for b, d in neighbours:
        remote(raw_target.at[T0], raw_target.at[b], rt_send, rt_recv, z_dev(d, False))
        remote(raw.at[T0], raw.at[b], raw_ssem.at[b], raw_rsem.at[b], z_dev(d, False))
    for q in range(1, n):
        pack_chunk(q)
        send_chunk(q)

    def pack_direct(e):
        halves = []
        for b in DIRECT[e]:
            arrived(raw.at[b], raw_rsem.at[b])
            to = raw_target[b].astype(jnp.int32)
            rows = dot_nn(one_hot(iota((shards * padded, row_dev), 0) == to), raw[b])
            halves.append(rows.reshape(shards, padded, UNIT)[:, :capacity])
        rows = jnp.concatenate(halves, axis=1).astype(jnp.bfloat16)
        recv_buf[n + e][0] = rows[0]
        send_buf[n + e][1:] = rows[1:]
        send_chunk(n + e)

    arrived(meta_recv.at[pl.ds(1, shards - 1)], meta_rsem)
    got = meta_recv[...].reshape(shards, 128)
    lanes = iota((shards, 128), 1)
    count = jnp.sum(jnp.where((got > 0.0) & (lanes < 64), 1.0, 0.0), axis=1, keepdims=True)
    lower = iota((shards, shards), 1) < iota((shards, shards), 0)
    count_row = jnp.sum(
        jnp.where(iota((shards, shards), 0) == iota((shards, shards), 1), count, 0.0),
        axis=0,
        keepdims=True,
    )
    offset = jnp.sum(jnp.where(lower, count_row, 0.0), axis=1, keepdims=True).astype(jnp.int32)
    count = count.astype(jnp.int32)

    def place(units, h, offset=offset, count=count):
        rows = padded if units == 1 else units * capacity
        k = iota((shards, shards * rows), 1) - iota((shards, shards * rows), 0) * rows - h * capacity
        good = (k >= 0) & (k < count)
        where_to = jnp.sum(jnp.where(good, offset + k + 1, 0), axis=0, keepdims=True) - 1
        return one_hot(iota((row_dev, shards * rows), 0) == where_to)

    gathers = {}

    def compact(q):
        units = plan[q]
        for h in range(units):
            if (units, h) not in gathers:
                gathers[units, h] = place(units, h)
        arrived(recv_buf[q].at[pl.ds(1, shards - 1)], xy_recv.at[q])
        rows = recv_buf[q][...]
        rows = rows.reshape(rows.shape[0] * rows.shape[1], UNIT)
        for h in range(units):
            blk[T0, first[q] + h] = dot_nn(gathers[units, h], rows).astype(jnp.bfloat16)
            send_own(first[q] + h)

    def direct_places(e):
        places = []
        for h, b in enumerate(DIRECT[e]):
            packed = counts[b][:, :1].astype(jnp.int32)
            places.append(place(2, h, packed % 1024, packed // 1024))
        return places

    def compact_direct(e):
        arrived(recv_buf[n + e].at[pl.ds(1, shards - 1)], xy_recv.at[n + e])
        rows = recv_buf[n + e][...]
        rows = rows.reshape(rows.shape[0] * rows.shape[1], UNIT)
        for h, b in enumerate(DIRECT[e]):
            blk[b, last] = dot_nn(direct_gather[e][h], rows).astype(jnp.bfloat16)
            if b == TM1:
                if TM2 not in direct:
                    z_copy(TM1, TM2, last, 1, False)
                z_copy(TM1, UM1, last, 0, True)
            elif b == TP1 and TP2 not in direct:
                z_copy(TP1, TP2, last, -1, False)
            elif b == TM2:
                z_copy(TM2, UM2, last, 0, True)

    def z_copy(src_slot, dst_slot, u, d, o):
        remote(
            blk.at[src_slot, u],
            blk.at[dst_slot, u],
            z_send.at[dst_slot, u],
            z_recv.at[dst_slot, u],
            z_dev(d, o),
        )

    def z_wait(slot_no, u):
        arrived(blk.at[slot_no, u], z_recv.at[slot_no, u])

    def units_of(q):
        return range(first[q], first[q + 1])

    def send_own(u):
        if u != last:
            z_copy(T0, TM1, u, 1, False)
            z_copy(T0, TP1, u, -1, False)
        z_copy(T0, U0, u, 0, True)

    def forward(q):
        for u in units_of(q):
            if u == last:
                continue
            z_wait(TM1, u)
            z_copy(TM1, TM2, u, 1, False)
            z_copy(TM1, UM1, u, 0, True)
            z_wait(TP1, u)
            z_copy(TP1, TP2, u, -1, False)

    compact(0)

    member = iota((shards, row_dev), 1)
    from_src = (member >= offset) & (member < offset + count)
    within = iota((1, row_dev), 1) - jnp.sum(jnp.where(from_src, offset, 0), axis=0, keepdims=True)
    got_t = jnp.concatenate([got, jnp.zeros((128 - shards, 128), jnp.float32)], axis=0).T
    from_pad = jnp.concatenate(
        [one_hot(from_src, jnp.float32), jnp.zeros((128 - shards, row_dev), jnp.float32)], axis=0
    )
    spread = dot_nn(got_t, from_pad, HIGHEST)
    key_row = jnp.sum(jnp.where(lane_k == within, spread, 0.0), axis=0, keepdims=True) - 1.0
    home_row = jnp.sum(jnp.where(lane_k == within + 64, spread, 0.0), axis=0, keepdims=True) - 1.0
    counts[T0] = jnp.broadcast_to((offset + 1024 * count).astype(jnp.float32), (shards, 128))
    for b, d in neighbours:
        remote(counts.at[T0], counts.at[b], c_send, c_recv, z_dev(d, False))
    source = jnp.sum(jnp.where(from_src, iota((shards, row_dev), 0), 0), axis=0, keepdims=True)
    zmeta[T0] = jnp.concatenate(
        [key_row, source.astype(jnp.float32) * row_dev + home_row], axis=0
    )
    for slot_no, d, o in (
        (TP1, -1, False),
        (TM1, 1, False),
        (TP2, -2, False),
        (TM2, 2, False),
        (U0, 0, True),
        (UM1, 1, True),
        (UM2, 2, True),
    ):
        remote(zmeta.at[T0], zmeta.at[slot_no], zm_send, zm_recv, z_dev(d, o))

    if DIRECT:
        arrived(raw_target.at[pl.ds(1, len(direct))], rt_recv)
    for q in range(1, n):
        compact(q)
        if q == 1:
            for e in range(len(DIRECT)):
                pack_direct(e)
        forward(q - 1)
        if q == PREPARE:
            home = one_hot(iota((row_dev, row_dev), 0) == home_row.astype(jnp.int32))
            arrived(zmeta.at[pl.ds(1, 7)], zm_recv)
            keys = zmeta[:, 0, :]
            late_src, late_home = [], []
            for b, _, _ in LATE:
                code = zmeta[b, 1:2, :].astype(jnp.int32)
                late_src.append(iota((shards, row_dev), 0) == code // row_dev)
                late_home.append(one_hot(iota((row_dev, row_dev), 0) == code % row_dev))
            eye = one_hot(iota((row_dev, row_dev), 0) == iota((row_dev, row_dev), 1), jnp.float32)
            keys_t = dot_nt(eye, keys, HIGHEST)
            for b in range(8):
                kcol[b] = jnp.broadcast_to(keys_t[:, b : b + 1], (row_dev, 128))
            first_key = jnp.floor(keys * (1.0 / RANKS)) * RANKS
            if DIRECT:
                arrived(counts.at[pl.ds(1, len(direct))], c_recv)
            direct_gather = [direct_places(e) for e in range(len(DIRECT))]
    if DIRECT:
        compact_direct(0)
    forward(n - 1)

    def scores(query, key, start, stop):
        total = None
        for u in range(start, stop, 2):
            take = range(u, min(u + 2, stop))
            a = jnp.concatenate([blk[key, v] for v in take], axis=1)
            b = jnp.concatenate([blk[query, v] for v in take], axis=1)
            term = dot_nt(a, b)
            total = term if total is None else total + term
        return total

    def top(query, key, total):
        col = jnp.concatenate([kcol[key]] * (row_dev // 128), axis=1)
        allowed = (col < keys[query : query + 1]) & (col >= first_key[query : query + 1])
        return jnp.max(jnp.where(allowed, total, -1.0), axis=0, keepdims=True)

    def best(query, key_slots):
        running = None
        for key in key_slots:
            found = top(query, key, scores(query, key, 0, first[n]))
            running = found if running is None else jnp.maximum(running, found)
        return running

    def send_part(p, value, d, o):
        part_send[p] = value
        remote(part_send.at[p], part_recv.at[p], p_send, p_recv, z_dev(d, o))

    all_units = range(first[n])
    tail = first[n] - 2

    def pass_on(units):
        for u in units:
            z_wait(TM2, u)
            z_copy(TM2, UM2, u, 0, True)

    pass_on(range(first[n - 2]))
    for u in all_units:
        z_wait(U0, u)
    mine = best(T0, (T0, U0, TP1))
    send_part(PU0, best(U0, (TP1,)), 0, True)
    early_p1 = best(TP1, (T0, U0, TM1))
    early_m1 = best(TM1, (TP1,))
    for u in all_units:
        z_wait(UM1, u)
    send_part(PP1, jnp.maximum(early_p1, best(TP1, (UM1,))), 1, False)
    early_um1 = best(UM1, (TP1,))

    def give_back(group, value, chosen, rows, d, o):
        back = dot_whole(jnp.where(chosen, value, 0.0), rows)
        ret_send[group] = back.reshape(shards, 1, row_dev)
        for k in range(shards):
            if group == 0 and k == 0:
                continue
            plane, _ = xy_dev(k, -1)
            remote(
                ret_send.at[group, k],
                ret_recv.at[group, k],
                r_send.at[group],
                r_recv.at[group],
                (plane, z_dev(d, o)[1]),
            )
        if group == 0:
            ret_recv[0, 0] = back[0:1]

    def give_late(group, value):
        _, d, o = LATE[group - 1]
        give_back(group, value, late_src[group - 1], late_home[group - 1], d, o)
    pass_on(range(first[n - 2], tail))
    if len(DIRECT) > 1:
        compact_direct(1)

    for u in range(tail):
        z_wait(TP2, u)
    pairs = ((TM1, TP2), (UM1, TP2), (TP2, TM1), (TP2, UM1), (TP2, TM2), (TP2, UM2))
    for a, (query, key) in enumerate(pairs):
        if key == UM2:
            for u in range(tail):
                z_wait(UM2, u)
        acc[a] = scores(query, key, 0, tail)

    def finish(a):
        query, key = pairs[a]
        return top(query, key, acc[a] + scores(query, key, tail, first[n]))

    by_z = range(tail, last if TM2 in direct else first[n])
    pass_on(by_z)
    for u in by_z:
        z_wait(TP2, u)
    late_m1 = jnp.maximum(early_m1, finish(0))
    late_um1 = jnp.maximum(early_um1, finish(1))
    late = jnp.maximum(jnp.maximum(finish(2), finish(3)), finish(4))
    for u in range(tail, first[n]):
        z_wait(UM2, u)
    give_late(3, jnp.maximum(late, finish(5)))
    give_late(1, late_m1)
    give_late(2, late_um1)

    arrived(part_recv, p_recv)
    mine = jnp.maximum(mine, jnp.max(part_recv[...].reshape(2, row_dev), axis=0, keepdims=True))
    give_back(0, mine, from_src, home, 0, False)

    arrived(ret_recv.at[0, pl.ds(1, shards - 1)], r_recv.at[0])
    for group in range(1, 1 + len(LATE)):
        arrived(ret_recv.at[group], r_recv.at[group])
    found = jnp.sum(ret_recv[...].reshape(1 + len(LATE), shards, row_dev), axis=1)
    out_ref[...] = jnp.max(found, axis=0, keepdims=True)

    arrived(meta_send.at[pl.ds(1, shards - 1)], meta_ssem)
    for q in range(m):
        arrived(send_buf[q].at[pl.ds(1, shards - 1)], xy_send.at[q])
    for u in all_units:
        for b in range(1, 8):
            if u == last and (b in direct):
                continue
            arrived(blk.at[b, u], z_send.at[b, u])
    for b, _ in neighbours:
        arrived(raw.at[b], raw_ssem.at[b])
    if DIRECT:
        arrived(raw_target.at[pl.ds(1, len(direct))], rt_send)
    if DIRECT:
        arrived(counts.at[pl.ds(1, len(direct))], c_send)
    arrived(zmeta.at[pl.ds(1, 7)], zm_send)
    arrived(part_send, p_send)
    arrived(ret_send.at[0, pl.ds(1, shards - 1)], r_send.at[0])
    for group in range(1, 1 + len(LATE)):
        arrived(ret_send.at[group], r_send.at[group])


def per_device(embedding, cluster_id, member_order):
    shards = lax.axis_size("shard")
    row_dev, depth = embedding.shape
    capacity = 5 * row_dev // (2 * shards)
    padded = -(-capacity // 16) * 16
    plan = PLAN
    n = len(plan)
    dma = pltpu.SemaphoreType.DMA
    vmem = pltpu.VMEM
    bf16, f32 = jnp.bfloat16, jnp.float32
    messages = [
        vmem((shards, padded if units == 1 else units * capacity, UNIT), bf16)
        for units in plan + (2,) * len(DIRECT)
    ]
    out = pl.pallas_call(
        functools.partial(kernel, shards, capacity, plan),
        out_shape=jax.ShapeDtypeStruct((1, row_dev), f32),
        in_specs=[pl.BlockSpec(memory_space=pltpu.HBM)] + [pl.BlockSpec(memory_space=vmem)] * 2,
        out_specs=pl.BlockSpec(memory_space=vmem),
        scratch_shapes=messages
        + messages
        + [
            vmem((row_dev, depth), bf16),
            vmem((8, depth // UNIT, row_dev, UNIT), bf16),
            vmem((6, row_dev, row_dev), f32),
            vmem((shards, 1, 128), f32),
            vmem((shards, 1, 128), f32),
            vmem((8, 2, row_dev), f32),
            vmem((5, row_dev, UNIT), bf16),
            vmem((5, 1, row_dev), f32),
            vmem((5, shards, 128), f32),
            vmem((8, row_dev, 128), f32),
            vmem((2, 1, row_dev), f32),
            vmem((2, 1, row_dev), f32),
            vmem((1 + len(LATE), shards, 1, row_dev), f32),
            vmem((1 + len(LATE), shards, 1, row_dev), f32),
            dma,
            dma((n + len(DIRECT),)),
            dma((n + len(DIRECT),)),
            dma,
            dma,
            dma((8, depth // UNIT)),
            dma((8, depth // UNIT)),
            dma,
            dma,
            dma((5,)),
            dma((5,)),
            dma,
            dma,
            dma,
            dma,
            dma,
            dma,
            dma((1 + len(LATE),)),
            dma((1 + len(LATE),)),
        ],
        compiler_params=pltpu.CompilerParams(
            collective_id=0, has_side_effects=True, vmem_limit_bytes=215 * 2**18
        ),
    )(embedding, cluster_id.reshape(1, row_dev), member_order.reshape(1, row_dev))
    return out.reshape(row_dev)


def solution(mesh):
    in_specs = (P(("shard", "grp"), None), P(("shard", "grp")), P(("shard", "grp")))
    out_specs = P(("shard", "grp"))
    return jax.shard_map(
        per_device, mesh=mesh, in_specs=in_specs, out_specs=out_specs, check_vma=False
    )
```
